128 devices in a mesh: ctx: 8 (over y, x_lo), dp: 16 (over z, x_hi, core).
Axes of the slice: x: 4 (x_hi: 2, x_lo: 2; x = x_hi * 2 + x_lo), y: 4, z: 4, core: 2. Of those that a mesh axis runs over, the one named last changes fastest.
Arguments:
- layer_input: bfloat16 [16, 4096, 4096], P('dp', 'ctx'), may hold values from -8 to 8
- grad_out: bfloat16 [16, 4096, 4096], P('dp', 'ctx'), may hold values from -0.25 to 0.25
- w_in: bfloat16 [4096, 1024], P(('ctx', 'dp')), may hold values from -0.09375 to 0.09375
- w_out_t: bfloat16 [4096, 256], P(('ctx', 'dp')), may hold values from -0.375 to 0.375
- decay_rate: float32 [128], replicated, may hold values from 2.4414063e-05 to 0.0625
Outputs:
- grad_input: bfloat16 [16, 4096, 4096], P('dp', 'ctx')
- grad_w_in: float32 [4096, 1024], P(('ctx', 'dp'))
- grad_w_out_t: float32 [4096, 256], P(('ctx', 'dp'))
The draws below stay inside these ranges and needn't reach their ends.
All inputs are finite; a program needn't handle non-finite values.
Results may differ from the reference program's by a relative error of at most 0.02.
Values may be sent and summed in bfloat16 or wider, within the bound.
A program may use at most 192 MiB of HBM per device.

```python
import math
import jax
import jax.numpy as jnp
from jax import lax

D = 4096
HEAD = 256
HALF = 128
BLOCK = 256
SEQ_LEN = 4096
SEQS = 16


def draw_decay_rate(key, part):
    lowest = 0.1 / SEQ_LEN
    highest = 1.0 / 16.0
    uniform_draw = jax.random.uniform(key, (HALF,), jnp.float32)
    rates = jnp.exp(math.log(lowest) + uniform_draw * (math.log(highest) - math.log(lowest)))
    return rates.astype(jnp.float32)


def with_spikes(entries, own_key, source, target, shards_of, factor):
    owner, partner = [(jnp.arange(entries.shape[dim]) // (entries.shape[dim] // shards_of)).reshape([-1 if axis == dim else 1 for axis in range(entries.ndim)]) for dim in (source, target)]
    chosen = jax.random.permutation(own_key, shards_of)[partner]
    strong = (owner == chosen) | (owner == (partner + shards_of // 2) % shards_of)
    return jnp.where(strong, factor * entries, entries)


def level_of(key, extent, shards, smallest, largest):
    gain = 1.0
    for axis_at, shards_of in shards:
        steps = jax.random.uniform(jax.random.fold_in(jax.random.fold_in(key, 6), axis_at), (shards_of,), jnp.float32, smallest / len(shards), largest / len(shards))
        gain = gain * jnp.repeat(jnp.exp(steps), extent[axis_at] // shards_of).reshape((-1,) + (1,) * (len(extent) - 1 - axis_at))
    return gain


def normal_values(stream_key, dims, deviation, most, pieces=(), kind=jnp.bfloat16):
    result = jax.random.normal(stream_key, dims, jnp.float32) * deviation
    if len(pieces) > 0:
        result = level_of(stream_key, dims, pieces, -0.22, 0.18) * result
    return jnp.clip(result, min=-most, max=most).astype(kind)


def gaussian_with(key, shape, scale, reach, cuts, heavy, held_as=jnp.bfloat16):
    entries = scale * jax.random.normal(key, shape, jnp.float32)
    if cuts:
        entries = entries * level_of(key, shape, cuts, -0.22, 0.18)
    return jnp.clip(with_spikes(entries, jax.random.fold_in(key, 3), *heavy), -reach, reach).astype(held_as)


def setup_inputs(seed: int = 0) -> dict:
    seeds = jax.random.split(jax.random.key(seed), 6)
    layer_input = gaussian_with(seeds[0], (SEQS, SEQ_LEN, D), 1.0, 8.0, ((0, 16), (1, 8)), (1, 2, 8, 2.0))
    grad_out = gaussian_with(seeds[1], (SEQS, SEQ_LEN, D), 0.03125, 0.25, ((0, 16), (1, 8)), (1, 2, 8, 2.0))
    w_in = normal_values(seeds[2], (D, 4 * HEAD), D ** -0.5, 0.09375, ((0, 128),))
    w_out_t = normal_values(seeds[3], (D, HEAD), HEAD ** -0.5, 0.375, ((0, 128),))
    decay_rate = draw_decay_rate(jax.random.fold_in(seeds[5], 71), 0)
    return dict(layer_input=layer_input, grad_out=grad_out, w_in=w_in, w_out_t=w_out_t, decay_rate=decay_rate)


EPSILON = 1e-06
HIGHEST = lax.Precision.HIGHEST

def rope_tables(first_row, row_count, half_width):
    position = (first_row + jnp.arange(row_count)).astype(jnp.float32)
    spacing = jnp.exp(jnp.arange(half_width).astype(jnp.float32) * (-math.log(10000.0) / half_width))
    angles = position[:, None] * spacing[None, :]
    return (jnp.cos(angles), jnp.sin(angles))

def rotate(values_in, cosine, sine):
    half_width = cosine.shape[1]
    leading = values_in[:, :half_width].astype(jnp.float32)
    trailing = values_in[:, half_width:].astype(jnp.float32)
    return jnp.concatenate([leading * cosine - trailing * sine, leading * sine + trailing * cosine], axis=1)

def unrotate(values_in, cosine, sine):
    half_width = cosine.shape[1]
    leading = values_in[:, :half_width]
    trailing = values_in[:, half_width:]
    return jnp.concatenate([leading * cosine + trailing * sine, trailing * cosine - leading * sine], axis=1)

def gate_norm(retained, gate_pre, grad_hidden):
    mean_sq = lax.optimization_barrier(jnp.mean(retained * retained, axis=1, keepdims=True))
    inverse = lax.rsqrt(mean_sq + EPSILON)
    normed = retained * inverse
    gate_f = gate_pre.astype(jnp.float32)
    sigmoid_g = jax.nn.sigmoid(gate_f)
    hidden = (gate_f * sigmoid_g * normed).astype(jnp.bfloat16)
    grad_normed = grad_hidden * gate_f * sigmoid_g
    grad_gate = grad_hidden * normed * sigmoid_g * (1.0 + gate_f * (1.0 - sigmoid_g))
    grad_ret = (inverse * (grad_normed - normed * lax.optimization_barrier(jnp.mean(grad_normed * normed, axis=1, keepdims=True)))).astype(jnp.bfloat16)
    return (hidden, grad_gate, grad_ret)

def decay_terms(rates):
    offsets = jnp.arange(BLOCK).astype(jnp.float32)
    delta = offsets[:, None] - offsets[None, :]
    weights = jnp.where(delta[:, :, None] >= 0.0, jnp.exp(-jnp.maximum(delta, 0.0)[:, :, None] * rates[None, None, :]), 0.0)
    column = offsets[:, None]
    enter_state = jnp.exp(-(column + 1.0) * rates[None, :])
    fade_out = jnp.exp(-(BLOCK - 1.0 - column) * rates[None, :])
    leave_state = jnp.exp(-(BLOCK - column) * rates[None, :])
    from_start = jnp.exp(-column * rates[None, :])
    block_decay = jnp.exp(-BLOCK * rates)
    return (weights, enter_state, fade_out, leave_state, from_start, block_decay)

def retention_grads(q_rot, k_rot, values_in, grad_fn, rates):
    weights, enter_state, fade_out, leave_state, from_start, block_decay = decay_terms(rates)
    head = q_rot.shape[1]
    blocks = q_rot.shape[0] // BLOCK
    query_blocks = q_rot.reshape(blocks, BLOCK, head).astype(jnp.float32)
    key_blocks = k_rot.reshape(blocks, BLOCK, head).astype(jnp.float32)
    value_blocks = values_in.reshape(blocks, BLOCK, head).astype(jnp.float32)

    def forward_step(state, block):
        query_full, key_full, value_full = block
        scores = jnp.einsum('ni,mi,nmi->nm', query_full, key_full, weights, precision=HIGHEST)
        retained = jnp.dot(scores, value_full, precision=HIGHEST) + jnp.dot(query_full * enter_state, state, precision=HIGHEST)
        new_state = block_decay[:, None] * state + jnp.dot((key_full * fade_out).T, value_full, precision=HIGHEST)
        return (new_state, (retained, state))
    zero_state = jnp.zeros((head, head), jnp.float32)
    _, (retained_blocks, state_blocks) = lax.scan(forward_step, zero_state, (query_blocks, key_blocks, value_blocks))
    retained = retained_blocks.reshape(blocks * BLOCK, head)
    hidden, grad_gate, grad_ret = grad_fn(retained)
    grad_blocks = grad_ret.reshape(blocks, BLOCK, head).astype(jnp.float32)

    def backward_step(grad_state, block):
        query_full, key_full, value_full, grad_full, state = block
        scores = jnp.einsum('ni,mi,nmi->nm', query_full, key_full, weights, precision=HIGHEST)
        score_grad = jnp.dot(grad_full, value_full.T, precision=HIGHEST)
        grad_query = jnp.einsum('nm,mi,nmi->ni', score_grad, key_full, weights, precision=HIGHEST) + jnp.dot(grad_full, state.T, precision=HIGHEST) * enter_state
        grad_key = jnp.einsum('nm,ni,nmi->mi', score_grad, query_full, weights, precision=HIGHEST) + jnp.dot(value_full, grad_state.T, precision=HIGHEST) * leave_state
        grad_value = jnp.dot(scores.T, grad_full, precision=HIGHEST) + jnp.dot(key_full * leave_state, grad_state, precision=HIGHEST)
        new_grad_state = block_decay[:, None] * grad_state + jnp.dot((query_full * from_start).T, grad_full, precision=HIGHEST)
        return (new_grad_state, (grad_query, grad_key, grad_value))
    _, (grad_q_blocks, grad_k_blocks, grad_v_blocks) = lax.scan(backward_step, zero_state, (query_blocks, key_blocks, value_blocks, grad_blocks, state_blocks), reverse=True)
    total_rows = blocks * BLOCK
    return (hidden, grad_gate, grad_q_blocks.reshape(total_rows, head), grad_k_blocks.reshape(total_rows, head), grad_v_blocks.reshape(total_rows, head))

def sequence_grads(tokens, upstream, w_in, w_out_t, rates, cosine, sine):
    head = w_out_t.shape[1]
    proj = jnp.dot(tokens, w_in, preferred_element_type=jnp.float32).astype(jnp.bfloat16)
    queries = proj[:, :head]
    keys_in = proj[:, head:2 * head]
    values_in = proj[:, 2 * head:3 * head]
    gate_pre = proj[:, 3 * head:]
    q_rot = rotate(queries, cosine, sine).astype(jnp.bfloat16)
    k_rot = rotate(keys_in, cosine, sine).astype(jnp.bfloat16)
    grad_hidden = jnp.dot(upstream, w_out_t, preferred_element_type=jnp.float32)

    def grad_fn(retained):
        return gate_norm(retained, gate_pre, grad_hidden)
    hidden, grad_gate, grad_qrot, grad_krot, grad_values = retention_grads(q_rot, k_rot, values_in, grad_fn, rates)
    grad_proj = jnp.concatenate([unrotate(grad_qrot, cosine, sine), unrotate(grad_krot, cosine, sine), grad_values, grad_gate], axis=1).astype(jnp.bfloat16)
    grad_tokens = lax.dot_general(grad_proj, w_in, (((1,), (1,)), ((), ())), preferred_element_type=jnp.float32).astype(jnp.bfloat16)
    grad_in = lax.dot_general(tokens, grad_proj, (((0,), (0,)), ((), ())), preferred_element_type=jnp.float32)
    grad_outw = lax.dot_general(upstream, hidden, (((0,), (0,)), ((), ())), preferred_element_type=jnp.float32)
    return (grad_tokens, grad_in, grad_outw)

def reference(layer_input, grad_out, w_in, w_out_t, decay_rate):
    rates = jnp.concatenate([decay_rate, decay_rate]).astype(jnp.float32)
    cosine, sine = rope_tables(0, layer_input.shape[1], decay_rate.shape[0])

    def per_sequence(totals, pair):
        tokens, upstream = pair
        grad_tokens, grad_in, grad_outw = sequence_grads(tokens, upstream, w_in, w_out_t, rates, cosine, sine)
        return ((totals[0] + grad_in, totals[1] + grad_outw), grad_tokens)
    start_totals = (jnp.zeros(w_in.shape, jnp.float32), jnp.zeros(w_out_t.shape, jnp.float32))
    (grad_w_in, grad_w_out_t), grad_input = lax.scan(per_sequence, start_totals, (layer_input, grad_out))
    return (grad_input, grad_w_in, grad_w_out_t)
```

```python
import math

import jax
import jax.numpy as jnp
from jax import lax
from jax.experimental import pallas as pl
from jax.experimental.pallas import tpu as pltpu
from jax.sharding import PartitionSpec as P

EPSILON = 1e-06
MESH = pl.DeviceIdType.MESH
F32, BF16 = jnp.float32, jnp.bfloat16
ROWS, WIDTH, HEAD, HALF = 512, 4096, 256, 128
CENTER = ROWS // 2
Q, K, V, GATE, OUT = range(5)
EVERY = slice(None)
ORDERS = (("x", "y", "z"), ("y", "z", "x"), ("z", "x", "y"))
GATHER = [(g, h) for g in (K, V, Q, GATE, OUT) for h in (0, 1)]
REDUCE = [(g, h) for g in (OUT, GATE, Q, K, V) for h in (0, 1)]
SPLIT = {"x": "y", "y": "z", "z": "y"}
BLOCK_DIMS = {"x": (4, 4), "y": (2, 4, 2), "z": (4, 2, 2)}
PART_DIMS = {"x": (4,), "y": (4,), "z": (2, 2)}
COUNT = 4


def dot(a, b, ca, cb):
    return lax.dot_general(a, b, (((ca,), (cb,)), ((), ())), preferred_element_type=F32)


def place(half=None, x=None, y=None, z=None):
    where = {"y": EVERY if y is None else y, "z": EVERY if z is None else z}
    if half is not None:
        where[half[0]] = pl.ds(2 * half[1], 2)
    if x is None:
        return (where["y"], EVERY, where["z"], EVERY)
    return (where["y"], lax.rem(x, 2), where["z"], lax.div(x, 2))


def body(x_hbm, u_hbm, win_hbm, wout_hbm, rate_ref, gin_hbm, gwin_ref, gwout_ref,
         xv, uv, xt, ut, wg, pr, pb, sb, gp, cos_ref, sin_ref, up_ref, down_ref, qs_ref, ks_ref, v_ref, score_ref, acc_ref,
         st, gs, hid_ref, gret_ref, stage,
         tx, ty, tz, bx, by, bz, cx, cy, cz, last,
         ag_s, ag_r, st_s, st_r, gs_s, gs_r, sib_s, sib_r, rs_s, rs_r, x_sem, u_sem, w_sem, out_sem):
    ctx, dp = lax.axis_index("ctx"), lax.axis_index("dp")
    core = lax.rem(dp, 2)
    here = {
        "x": lax.rem(lax.div(dp, 2), 2) * 2 + lax.rem(ctx, 2),
        "y": lax.div(ctx, 2),
        "z": lax.div(dp, 4),
    }

    def device(at, on_core):
        return (at["y"] * 2 + lax.rem(at["x"], 2), at["z"] * 4 + lax.div(at["x"], 2) * 2 + on_core)

    def shifted(axis, by):
        return lax.rem(here[axis] + by, 4)

    def peer(axis, by):
        return device({**here, axis: shifted(axis, by)}, core)

    sibling = (ctx, dp + 1 - 2 * core)

    def remote(src, dst, send, recv, to):
        return pltpu.make_async_remote_copy(
            src_ref=src, dst_ref=dst, send_sem=send, recv_sem=recv, device_id=to, device_id_type=MESH
        )

    loads = []
    for c in range(4):
        lanes = pl.ds(c * 1024, 1024)
        for src, dst, sem in ((x_hbm, xv, x_sem), (u_hbm, uv, u_sem)):
            copy = pltpu.make_async_copy(src.at[:, lanes], dst.at[:, lanes], sem.at[c])
            loads.append(copy)
    own = []
    for n, (g, h) in enumerate(GATHER):
        rows = pl.ds(16 * h, 16)
        src = wout_hbm.at[rows] if g == OUT else win_hbm.at[rows, pl.ds(g * HEAD, HEAD)]
        copy = pltpu.make_async_copy(src, wg.at[(g,) + place(**here) + (core, h)], w_sem.at[n])
        copy.start()
        own.append(copy)
    for copy in loads:
        copy.start()

    greeted = [peer(axis, by) for axis in "xyz" for by in (1, 2, 3)] + [sibling]
    crossed = here["x"] + 1 - 2 * lax.rem(here["x"], 2)
    greeted += [device({**here, "x": crossed, "y": shifted("y", by)}, core) for by in (1, 2, 3)]
    barrier = pltpu.get_barrier_semaphore()
    for to in greeted:
        pl.semaphore_signal(barrier, inc=1, device_id=to, device_id_type=MESH)
    pl.semaphore_wait(barrier, len(greeted))

    unsent = []

    def send(src, dst, send_sem, recv_sem, to):
        copy = remote(src, dst, send_sem, recv_sem, to)
        copy.start()
        unsent.append(copy)

    def arrived(ref, recv_sem, spare):
        remote(ref, ref, spare, recv_sem, sibling).wait_recv()

    def w_at(n, **fixed):
        g, h = GATHER[n]
        return wg.at[(g,) + place(**fixed) + (core, h)]

    def ag_send(n, k, to, **fixed):
        send(w_at(n, **fixed), w_at(n, **fixed), ag_s.at[n, k], ag_r.at[n, k], to)

    def ag_wait(n, k, **fixed):
        arrived(w_at(n, **fixed), ag_r.at[n, k], ag_s.at[n, k])

    def fixed_from(order, first):
        return {a: here[a] for a in order[first:]}

    def ag_spread(n, phase):
        order = ORDERS[n % 3]
        axis, fixed = order[phase], fixed_from(order, phase)
        for k, by in enumerate((1, 3, 2)):
            ag_send(n, 3 * phase + k, peer(axis, by), **fixed)

    def ag_spread_wait(n, phase):
        order = ORDERS[n % 3]
        axis, fixed = order[phase], fixed_from(order, phase)
        for k, by in enumerate((3, 1, 2)):
            ag_wait(n, 3 * phase + k, **{**fixed, axis: shifted(axis, by)})

    def ag_last(n):
        axis = ORDERS[n % 3][2]
        ag_send(n, 6, peer(axis, 1), **{axis: here[axis]})
        ag_send(n, 7, peer(axis, 3), **{axis: here[axis]})

    def ag_relay(n):
        axis = ORDERS[n % 3][2]
        left, right = shifted(axis, 3), shifted(axis, 1)
        ag_wait(n, 6, **{axis: left})
        ag_send(n, 8, peer(axis, 1), half=(SPLIT[axis], 0), **{axis: left})
        ag_wait(n, 7, **{axis: right})
        ag_send(n, 9, peer(axis, 3), half=(SPLIT[axis], 1), **{axis: right})

    def ag_opposite(n):
        axis = ORDERS[n % 3][2]
        far = shifted(axis, 2)
        ag_wait(n, 8, half=(SPLIT[axis], 0), **{axis: far})
        ag_wait(n, 9, half=(SPLIT[axis], 1), **{axis: far})
        ag_send(n, 10, sibling)

    def ag_done(n):
        g, h = GATHER[n]
        arrived(wg.at[(g,) + place() + (1 - core, h)], ag_r.at[n, 10], ag_s.at[n, 10])

    units = range(len(GATHER))
    for copy in own:
        copy.wait()
    for n in units:
        ag_spread(n, 0)

    rate = rate_ref[...]
    row = lax.broadcasted_iota(jnp.int32, (ROWS, HALF), 0).astype(F32)
    spacing = jnp.exp(
        lax.broadcasted_iota(jnp.int32, (1, HALF), 1).astype(F32) * (-math.log(10000.0) / HALF)
    )
    angle = (row + (ctx * ROWS).astype(F32)) * spacing
    cos_ref[...] = jnp.cos(angle)
    sin_ref[...] = jnp.sin(angle)
    up_ref[...] = jnp.exp((CENTER - row) * rate)
    down_ref[...] = jnp.exp((row - CENTER) * rate)
    rates = jnp.concatenate([rate, rate], axis=1)

    for n in units:
        ag_spread_wait(n, 0)
        ag_spread(n, 1)
    waves = [units[0:4], units[4:8], units[8:10]]
    for n in units:
        ag_spread_wait(n, 1)
        if n in waves[0]:
            ag_last(n)
    for copy in loads:
        copy.wait()

    def transpose(src, dst):
        def step(c, _):
            at = pl.ds(pl.multiple_of(c * 256, 256), 256)
            dst[at, :] = src[:, at].T
            return _
        lax.fori_loop(0, WIDTH // 256, step, 0)

    transpose(xv, xt)
    for n in waves[0]:
        ag_relay(n)
    for n in waves[1]:
        ag_last(n)
    transpose(uv, ut)
    for n in waves[0]:
        ag_opposite(n)

    def project(g):
        for n, (group, _) in enumerate(GATHER):
            if group == g:
                ag_done(n)
        left = uv if g == OUT else xv
        pr[g] = dot(left[...], wg[g].reshape(WIDTH, HEAD), 1, 0)

    def rotated(a):
        a = a.astype(BF16).astype(F32)
        a1, a2 = a[:, :HALF], a[:, HALF:]
        cos, sin = cos_ref[...], sin_ref[...]
        return jnp.concatenate([a1 * cos - a2 * sin, a1 * sin + a2 * cos], axis=1).astype(BF16).astype(F32)

    def unrotated(g):
        g1, g2 = g[:, :HALF], g[:, HALF:]
        cos, sin = cos_ref[...], sin_ref[...]
        return jnp.concatenate([g1 * cos + g2 * sin, g2 * cos - g1 * sin], axis=1).astype(BF16)

    def twice(t):
        return jnp.concatenate([t, t], axis=1)

    for n in waves[1]:
        ag_relay(n)
    for n in waves[2]:
        ag_last(n)
    project(K)
    ks_ref[...] = (rotated(pr[K]) * twice(down_ref[...])).astype(BF16)
    project(V)
    v_ref[...] = pr[V].astype(BF16)
    st[ctx] = (dot(v_ref[...], ks_ref[...], 0, 0) * jnp.exp(-(CENTER - 1.0) * rates)).astype(BF16)

    def each_later(act):
        for d in range(1, 8):
            @pl.when(ctx + d < 8)
            def _():
                act(remote(st.at[ctx], st.at[ctx], st_s.at[d - 1], st_r.at[ctx], (ctx + d, dp)))

    each_later(lambda copy: copy.start())
    for n in waves[2]:
        ag_relay(n)
    for n in waves[1]:
        ag_opposite(n)
    project(Q)
    qs_ref[...] = (rotated(pr[Q]) * twice(up_ref[...])).astype(BF16)
    for n in waves[2]:
        ag_opposite(n)
    project(GATE)
    before = lax.broadcasted_iota(jnp.int32, (ROWS, ROWS), 0) >= lax.broadcasted_iota(jnp.int32, (ROWS, ROWS), 1)
    score_ref[...] = jnp.where(before, dot(qs_ref[...], ks_ref[...], 1, 1), 0.0).astype(BF16)
    project(OUT)

    shard_decay = jnp.exp(-float(ROWS) * rates)
    acc_ref[...] = jnp.zeros_like(acc_ref)

    def take(i, _):
        arrived(st.at[i], st_r.at[i], st_s.at[0])
        acc_ref[...] = acc_ref[...] * shard_decay + st[i].astype(F32)
        return _

    lax.fori_loop(0, ctx, take, 0)
    state = (acc_ref[...] * jnp.exp(-(CENTER + 1.0) * rates)).astype(BF16)

    retained = dot(score_ref[...], v_ref[...], 1, 0) + dot(qs_ref[...], state, 1, 1)
    inverse = lax.rsqrt(jnp.mean(retained * retained, axis=1, keepdims=True) + EPSILON)
    normed = retained * inverse
    gate = pr[GATE].astype(BF16).astype(F32)
    grad_hidden = pr[OUT]
    sig = jax.nn.sigmoid(gate)
    hid_ref[...] = (gate * sig * normed).astype(BF16)
    grad_normed = grad_hidden * gate * sig
    gp[:, GATE * HEAD:] = (grad_hidden * normed * sig * (1.0 + gate * (1.0 - sig))).astype(BF16)
    gret_ref[...] = (
        inverse * (grad_normed - normed * jnp.mean(grad_normed * normed, axis=1, keepdims=True))
    ).astype(BF16)

    gs[ctx] = (dot(gret_ref[...], qs_ref[...], 0, 0) * jnp.exp(-float(CENTER) * rates)).astype(BF16)

    def each_earlier(act):
        for d in range(1, 8):
            @pl.when(ctx - d >= 0)
            def _():
                act(remote(gs.at[ctx], gs.at[ctx], gs_s.at[d - 1], gs_r.at[ctx], (ctx - d, dp)))

    each_earlier(lambda copy: copy.start())

    def term(g):
        left = ut if g == OUT else xt

        def step(c, _):
            right = hid_ref[...] if g == OUT else gp[:, g * HEAD:(g + 1) * HEAD]
            rows = pl.ds(pl.multiple_of(c * 1024, 1024), 1024)
            pb[g, c] = dot(left[rows, :], right, 1, 0).astype(BF16).reshape(2, 4, 2, 2, 2, 16, HEAD)
            return _

        lax.fori_loop(0, 4, step, 0)
        send(pb.at[(g,) + place() + (1 - core,)], sb.at[g], sib_s.at[g], sib_r.at[g], sibling)

    def pair(g):
        arrived(sb.at[g], sib_r.at[g], sib_s.at[g])

        def step(c, _):
            mine = pb[g, c, :, :, :, core]
            sb[g, c] = (sb[g, c].astype(F32) + mine.astype(F32)).astype(BF16)
            return _

        lax.fori_loop(0, 4, step, 0)

    opposite = {"x": tx, "y": ty, "z": tz}
    blocks = {"x": bx, "y": by, "z": bz}
    parts = {"x": cx, "y": cy, "z": cz}

    def s_idx(n, **fixed):
        g, h = REDUCE[n]
        return (g,) + place(**fixed) + (h,)

    def t_at(n, side):
        axis = ORDERS[n % 3][2]
        half = pl.ds(2 * side, 2)
        return opposite[axis].at[(n // 3, EVERY, half) if axis == "y" else (n // 3, half)]

    def rs_first(n):
        axis = ORDERS[n % 3][2]
        far = shifted(axis, 2)
        for side, by in ((0, 1), (1, 3)):
            src = sb.at[s_idx(n, half=(SPLIT[axis], side), **{axis: far})]
            send(src, t_at(n, side), rs_s.at[n, side], rs_r.at[n, side], peer(axis, by))

    def rs_second(n):
        axis = ORDERS[n % 3][2]
        for side, by in ((0, 1), (1, 3)):
            arrived(t_at(n, side), rs_r.at[n, side], rs_s.at[n, side])
            at = s_idx(n, half=(SPLIT[axis], side), **{axis: shifted(axis, by)})
            sb[at] = (sb[at].astype(F32) + t_at(n, side)[...].astype(F32)).astype(BF16)
            send(sb.at[s_idx(n, **{axis: shifted(axis, by)})], blocks[axis].at[n // 3, side],
                 rs_s.at[n, 2 + side], rs_r.at[n, 2 + side], peer(axis, by))

    def rs_third(n):
        a1, a2, a3 = ORDERS[n % 3]
        for side in (0, 1):
            ref = blocks[a3].at[n // 3, side]
            arrived(ref, rs_r.at[n, 2 + side], rs_s.at[n, 2 + side])
        at = s_idx(n, **{a3: here[a3]})
        got = blocks[a3]
        sb[at] = (sb[at].astype(F32) + got[n // 3, 0].astype(F32) + got[n // 3, 1].astype(F32)).astype(BF16)
        for k, by in enumerate((1, 3, 2)):
            src = sb.at[s_idx(n, **{a3: here[a3], a2: shifted(a2, by)})]
            send(src, parts[a3].at[n // 3, k], rs_s.at[n, 4 + k], rs_r.at[n, 4 + k], peer(a2, by))

    def rs_fourth(n):
        a1, a2, a3 = ORDERS[n % 3]
        got = parts[a3]
        for k in range(3):
            arrived(got.at[n // 3, k], rs_r.at[n, 4 + k], rs_s.at[n, 4 + k])
        at = s_idx(n, **{a3: here[a3], a2: here[a2]})
        total = sb[at].astype(F32)
        for k in range(3):
            total += got[n // 3, k].astype(F32)
        sb[at] = total.astype(BF16)
        for k, by in enumerate((1, 3, 2)):
            src = sb.at[s_idx(n, **{a3: here[a3], a2: here[a2], a1: shifted(a1, by)})]
            send(src, last.at[n, k], rs_s.at[n, 7 + k], rs_r.at[n, 7 + k], peer(a1, by))

    def rs_end(n):
        g, h = REDUCE[n]
        for k in range(3):
            arrived(last.at[n, k], rs_r.at[n, 7 + k], rs_s.at[n, 7 + k])
        total = sb[s_idx(n, **here)].astype(F32)
        for k in range(3):
            total += last[n, k].astype(F32)
        if g == OUT:
            gwout_ref[16 * h:16 * h + 16, :] = total
        else:
            gwin_ref[16 * h:16 * h + 16, g * HEAD:(g + 1) * HEAD] = total

    puts = []

    def grad_input(c):
        slot = c % 2
        if c >= 2:
            puts[c - 2].wait()
        w = jnp.concatenate([wg[g, c].reshape(1024, HEAD) for g in (Q, K, V, GATE)], axis=1)
        stage[slot] = dot(gp[...], w, 1, 1).astype(BF16)
        put = pltpu.make_async_copy(stage.at[slot], gin_hbm.at[:, pl.ds(c * 1024, 1024)], out_sem.at[c])
        put.start()
        puts.append(put)

    term(OUT)
    term(GATE)
    score_grad = jnp.where(before, dot(gret_ref[...], v_ref[...], 1, 1), 0.0).astype(BF16)
    pr[Q] = dot(score_grad, ks_ref[...], 1, 0) + dot(gret_ref[...], state, 1, 0)
    pair(OUT)
    for n in (0, 1):
        rs_first(n)
    pr[K] = dot(score_grad, qs_ref[...], 0, 0)
    pair(GATE)
    for n in (2, 3):
        rs_first(n)
    gp[:, Q * HEAD:(Q + 1) * HEAD] = unrotated(pr[Q] * twice(up_ref[...]))
    term(Q)
    pr[V] = dot(score_ref[...], gret_ref[...], 0, 0)
    for n in (0, 1):
        rs_second(n)
    acc_ref[...] = jnp.zeros_like(acc_ref)

    def take_back(j, _):
        i = 7 - j
        arrived(gs.at[i], gs_r.at[i], gs_s.at[0])
        acc_ref[...] = acc_ref[...] * shard_decay + gs[i].astype(F32)
        return _

    lax.fori_loop(0, 7 - ctx, take_back, 0)
    grad_state = (acc_ref[...] * jnp.exp(-float(CENTER) * rates)).astype(BF16)
    gp[:, K * HEAD:(K + 1) * HEAD] = unrotated(
        (pr[K] + dot(v_ref[...], grad_state, 1, 0)) * twice(down_ref[...])
    )
    term(K)
    pair(Q)
    for n in (4, 5):
        rs_first(n)
    for n in (2, 3):
        rs_second(n)
    gp[:, V * HEAD:(V + 1) * HEAD] = (pr[V] + dot(ks_ref[...], grad_state, 1, 1)).astype(BF16)
    term(V)
    pair(K)
    for n in (6, 7):
        rs_first(n)
    pair(V)
    for n in (8, 9):
        rs_first(n)
    for n in (0, 1):
        rs_third(n)
    for n in (4, 5):
        rs_second(n)
    grad_input(0)
    for n in (2, 3):
        rs_third(n)
    for n in (6, 7):
        rs_second(n)
    for n in (8, 9):
        rs_second(n)
    grad_input(1)
    for n in (0, 1, 2, 3):
        rs_fourth(n)
    for n in (4, 5):
        rs_third(n)
    grad_input(2)
    for n in (6, 7, 8, 9):
        rs_third(n)
    grad_input(3)
    for n in (4, 5, 6, 7, 8, 9):
        rs_fourth(n)
    for n in range(10):
        rs_end(n)
    for put in puts[2:]:
        put.wait()
    for copy in unsent:
        copy.wait_send()
    each_later(lambda copy: copy.wait_send())
    each_earlier(lambda copy: copy.wait_send())


def on_device(layer_input, grad_out, w_in, w_out_t, decay_rate):
    hbm, vmem = pl.BlockSpec(memory_space=pl.ANY), pl.BlockSpec(memory_space=pltpu.VMEM)
    dma = pltpu.SemaphoreType.DMA
    buf = pltpu.VMEM
    grad_in, grad_w, grad_wo = pl.pallas_call(
        body,
        out_shape=(
            jax.ShapeDtypeStruct((ROWS, WIDTH), BF16),
            jax.ShapeDtypeStruct((32, 4 * HEAD), F32),
            jax.ShapeDtypeStruct((32, HEAD), F32),
        ),
        in_specs=[hbm, hbm, hbm, hbm, vmem],
        out_specs=(hbm, vmem, vmem),
        scratch_shapes=[
            buf((ROWS, WIDTH), BF16),
            buf((ROWS, WIDTH), BF16),
            buf((WIDTH, ROWS), BF16),
            buf((WIDTH, ROWS), BF16),
            buf((5, 4, 2, 4, 2, 2, 2, 16, HEAD), BF16),
            buf((5, ROWS, HEAD), F32),
            buf((5, 4, 2, 4, 2, 2, 2, 16, HEAD), BF16),
            buf((5, 4, 2, 4, 2, 2, 16, HEAD), BF16),
            buf((ROWS, 4 * HEAD), BF16),
            buf((ROWS, HALF), F32), buf((ROWS, HALF), F32), buf((ROWS, HALF), F32), buf((ROWS, HALF), F32),
            buf((ROWS, HEAD), BF16), buf((ROWS, HEAD), BF16), buf((ROWS, HEAD), BF16),
            buf((ROWS, ROWS), BF16),
            buf((HEAD, HEAD), F32),
            buf((8, HEAD, HEAD), BF16), buf((8, HEAD, HEAD), BF16),
            buf((ROWS, HEAD), BF16), buf((ROWS, HEAD), BF16),
            buf((2, ROWS, 1024), BF16),
            *[buf((COUNT,) + BLOCK_DIMS[a] + (16, HEAD), BF16) for a in "xyz"],
            *[buf((COUNT, 2) + BLOCK_DIMS[a] + (16, HEAD), BF16) for a in "xyz"],
            *[buf((COUNT, 3) + PART_DIMS[a] + (16, HEAD), BF16) for a in "xyz"],
            buf((10, 3, 16, HEAD), BF16),
            dma((10, 11)), dma((10, 11)),
            dma((7,)), dma((8,)), dma((7,)), dma((8,)),
            dma((5,)), dma((5,)),
            dma((10, 10)), dma((10, 10)),
            dma((4,)), dma((4,)), dma((10,)), dma((4,)),
        ],
        compiler_params=pltpu.CompilerParams(
            collective_id=0, has_side_effects=True, vmem_limit_bytes=62 * 1024 * 1024
        ),
        cost_estimate=pl.CostEstimate(flops=17 * 10**9, bytes_accessed=13 * 10**6, transcendentals=10**6),
        name="retention_backward",
    )(layer_input[0], grad_out[0], w_in, w_out_t, decay_rate[None, :])
    return grad_in[None], grad_w, grad_wo


def solution(mesh):
    rows = P(("ctx", "dp"), None)
    tokens = P("dp", "ctx", None)
    return jax.shard_map(
        on_device,
        mesh=mesh,
        in_specs=(tokens, tokens, rows, rows, P()),
        out_specs=(tokens, rows, rows),
        check_vma=False,
    )
```

```python
import math

import jax
import jax.numpy as jnp
from jax import lax
from jax.experimental import pallas as pl
from jax.experimental.pallas import tpu as pltpu
from jax.sharding import PartitionSpec as P

EPSILON = 1e-06
MESH = pl.DeviceIdType.MESH
F32, BF16 = jnp.float32, jnp.bfloat16
ROWS, WIDTH, HEAD, HALF = 512, 4096, 256, 128
CENTER = ROWS // 2
K, V, Q, GATE, OUT = range(5)
EVERY = slice(None)
ORDERS = (("x", "y", "z"), ("y", "z", "x"), ("z", "x", "y"))
PIECES = (
    (0, slice(0, 384), 256), (1, slice(0, 384), 256), (EVERY, slice(384, 512), 640),
    (EVERY, slice(512, 768), 0), (EVERY, slice(768, 1024), 768), (EVERY, slice(1024, 1280), None),
)
KV, QGO = (0, 1, 2), (3, 4, 5)
SPLIT = {"x": "y", "y": "z", "z": "y"}
BLOCK_DIMS = {"x": (4, 4), "y": (2, 4, 2), "z": (4, 2, 2)}
PART_DIMS = {"x": (4,), "y": (4,), "z": (2, 2)}


def inner(n):
    rows, lanes, _ = PIECES[n]
    return ((2,) if rows == EVERY else ()) + (16, lanes.stop - lanes.start)


def lanes_of(g):
    return slice(g * HEAD, (g + 1) * HEAD)


def dot(a, b, ca, cb):
    return lax.dot_general(a, b, (((ca,), (cb,)), ((), ())), preferred_element_type=F32)


def place(half=None, x=None, y=None, z=None):
    where = {"y": EVERY if y is None else y, "z": EVERY if z is None else z}
    if half is not None and half[0] != "x":
        where[half[0]] = pl.ds(2 * half[1], 2)
    if x is None:
        return (where["y"], EVERY, where["z"], pl.ds(half[1], 1) if half is not None and half[0] == "x" else EVERY)
    return (where["y"], lax.rem(x, 2), where["z"], lax.div(x, 2))


def body(x_hbm, u_hbm, win_hbm, wout_hbm, rate_ref, gin_hbm, gwin_ref, gwout_ref,
         xv, uv, xt, ut, wg, pr, pb, sb, gp, cos_ref, sin_ref, up_ref, down_ref, qs_ref, ks_ref, v_ref, score_ref, acc_ref,
         st, st_pair, st_y, st_sum, gs, gs_pair, gs_y, gs_sum, hid_ref, gret_ref, stage, *rest):
    far_a, near_a, far_b, near_b, last = (rest[6 * k:6 * k + 6] for k in range(5))
    ag_s, ag_r, st_s, st_r, gs_s, gs_r, sib_s, sib_r, rs_s, rs_r, load_sem, out_sem = rest[30:]
    ctx, dp = lax.axis_index("ctx"), lax.axis_index("dp")
    core = lax.rem(dp, 2)
    here = {
        "x": lax.rem(lax.div(dp, 2), 2) * 2 + lax.rem(ctx, 2),
        "y": lax.div(ctx, 2),
        "z": lax.div(dp, 4),
    }

    def device(at, on_core):
        return (at["y"] * 2 + lax.rem(at["x"], 2), at["z"] * 4 + lax.div(at["x"], 2) * 2 + on_core)

    def shifted(axis, by):
        return lax.rem(here[axis] + by, 4)

    def peer(axis, by):
        return device({**here, axis: shifted(axis, by)}, core)

    sibling = (ctx, dp + 1 - 2 * core)

    def remote(src, dst, send, recv, to):
        return pltpu.make_async_remote_copy(
            src_ref=src, dst_ref=dst, send_sem=send, recv_sem=recv, device_id=to, device_id_type=MESH
        )

    mine = place(**here) + (core,)
    own = wg.at[mine]
    for src, first, to, size in ((win_hbm, HEAD, K, 2), (win_hbm, 0, Q, 1), (win_hbm, 3 * HEAD, GATE, 1), (wout_hbm, 0, OUT, 1)):
        src = src.at[:, :, pl.ds(first, size * HEAD)]
        pltpu.make_async_copy(src, wg.at[mine + (EVERY, EVERY, pl.ds(to * HEAD, size * HEAD))], load_sem.at[2]).start()
    load_x = pltpu.make_async_copy(x_hbm, xv, load_sem.at[0])
    load_u = pltpu.make_async_copy(u_hbm, uv, load_sem.at[1])
    load_x.start()
    load_u.start()

    greeted = [peer(axis, by) for axis in "xyz" for by in (1, 2, 3)] + [sibling]
    barrier = pltpu.get_barrier_semaphore()
    for to in greeted:
        pl.semaphore_signal(barrier, inc=1, device_id=to, device_id_type=MESH)
    pl.semaphore_wait(barrier, len(greeted))

    def send(src, dst, send_sem, recv_sem, to):
        remote(src, dst, send_sem, recv_sem, to).start()

    def arrived(ref, recv_sem):
        remote(ref, ref, ag_s.at[0], recv_sem, sibling).wait_recv()

    def sent(ref, send_sem):
        remote(ref, ref, send_sem, ag_r.at[0, 0], sibling).wait_send()

    def w_at(n, **fixed):
        rows, lanes, _ = PIECES[n]
        return wg.at[place(**fixed) + (core, rows, EVERY, lanes)]

    W_BYTES = ((slice(0, 3), 0, 0, 0), (slice(0, 2), 0, EVERY, 0), (slice(0, 1), 0, EVERY, 0),
               (slice(0, 2), EVERY, EVERY, EVERY), (0, EVERY, EVERY, EVERY), (EVERY, EVERY, EVERY, EVERY))

    def ag_send(n, step, to, **fixed):
        send(w_at(n, **fixed), w_at(n, **fixed), ag_s.at[step], ag_r.at[n, step], to)

    def ag_wait(n, step):
        rows, lanes, _ = PIECES[n]
        arrived(wg.at[W_BYTES[step] + (0, rows, EVERY, lanes)], ag_r.at[n, step])

    def ag_first(n):
        axis = ORDERS[n % 3][0]
        for by in (1, 3, 2):
            ag_send(n, 0, peer(axis, by), **here)

    def ag_both(n, k):
        order = ORDERS[n % 3]
        axis, fixed = order[k], {a: here[a] for a in order[k:]}
        for by in (1, 3):
            ag_send(n, 2 * k - 1, peer(axis, by), **fixed)
        if k == 2:
            ag_send(n, 5, sibling, **fixed)

    def ag_relay(n, k):
        order = ORDERS[n % 3]
        axis, fixed = order[k], {a: here[a] for a in order[k:]}
        split = order[0] if k == 1 else SPLIT[axis]
        ag_wait(n, 2 * k - 1)
        for by, side in ((1, 0), (3, 1)):
            ag_send(n, 2 * k, peer(axis, by), half=(split, side), **{**fixed, axis: shifted(axis, 4 - by)})
        if k == 2:
            for by in (1, 3):
                ag_send(n, 5, sibling, **{**fixed, axis: shifted(axis, by)})

    def ag_opposite(n):
        axis = ORDERS[n % 3][2]
        ag_wait(n, 4)
        ag_send(n, 5, sibling, **{axis: shifted(axis, 2)})

    def ag_done(n):
        ag_wait(n, 5)

    pltpu.make_async_copy(own, own, load_sem.at[2]).wait()
    for n in KV + QGO:
        ag_first(n)

    rate = rate_ref[...]
    row = lax.broadcasted_iota(jnp.int32, (ROWS, HALF), 0).astype(F32)
    spacing = jnp.exp(
        lax.broadcasted_iota(jnp.int32, (1, HALF), 1).astype(F32) * (-math.log(10000.0) / HALF)
    )

    def make_tables():
        angle = (row + (ctx * ROWS).astype(F32)) * spacing
        cos_ref[...] = jnp.cos(angle)
        sin_ref[...] = jnp.sin(angle)
        up_ref[...] = jnp.exp((CENTER - row) * rate)
        down_ref[...] = jnp.exp((row - CENTER) * rate)

    rates = jnp.concatenate([rate, rate], axis=1)

    def transpose(src, dst):
        def step(c, _):
            at = pl.ds(pl.multiple_of(c * 512, 512), 512)
            dst[lax.div(c, 2), lax.rem(c, 2)] = src[:, at].T.reshape(4, 2, 2, 32, ROWS)
            return _
        lax.fori_loop(0, 8, step, 0)

    make_tables()
    for n in KV + QGO:
        ag_wait(n, 0)
        ag_both(n, 1)
    for n in KV + QGO:
        ag_relay(n, 1)
    for n in KV:
        ag_wait(n, 2)
        ag_both(n, 2)
    load_x.wait()
    transpose(xv, xt)
    for n in KV:
        ag_relay(n, 2)
    for n in QGO:
        ag_wait(n, 2)
        ag_both(n, 2)
    load_u.wait()
    transpose(uv, ut)
    for n in KV:
        ag_opposite(n)

    def project(g):
        left = uv if g == OUT else xv
        pr[g] = dot(left[...], wg[..., lanes_of(g)].reshape(WIDTH, HEAD), 1, 0)

    def rotated(a):
        a = a.astype(BF16).astype(F32)
        a1, a2 = a[:, :HALF], a[:, HALF:]
        cos, sin = cos_ref[...], sin_ref[...]
        return jnp.concatenate([a1 * cos - a2 * sin, a1 * sin + a2 * cos], axis=1).astype(BF16).astype(F32)

    def unrotated(g):
        g1, g2 = g[:, :HALF], g[:, HALF:]
        cos, sin = cos_ref[...], sin_ref[...]
        return jnp.concatenate([g1 * cos + g2 * sin, g2 * cos - g1 * sin], axis=1).astype(BF16)

    def twice(t):
        return jnp.concatenate([t, t], axis=1)

    x_low = lax.rem(ctx, 2)
    pair_at = (ctx + 1 - 2 * x_low, dp)
    my_half, pair_half = pl.ds(128 * x_low, 128), pl.ds(128 * (1 - x_low), 128)
    shard_decay = jnp.exp(-float(ROWS) * rates)
    pair_decay = jnp.exp(-2.0 * ROWS * rates)

    class Exchange:
        def __init__(self, own, other, along_y, total, send_sem, recv_sem, backward):
            self.own, self.other, self.along_y, self.total = own, other, along_y, total
            self.s, self.r = send_sem, recv_sem
            self.hears, self.tells = (x_low == 0, x_low == 1) if backward else (x_low == 1, x_low == 0)
            self.backward = backward
            self.to_pair = remote(own.at[pair_half], other.at[pair_half], self.s.at[0], self.r.at[0], pair_at)
            self.to_pair_rest = remote(own.at[my_half], other.at[my_half], self.s.at[1], self.r.at[1], pair_at)
            self.halves = remote(total.at[my_half], total.at[my_half], self.s.at[2], self.r.at[2], pair_at)

        def each_y(self, act):
            for d in range(1, 4):
                to = here["y"] - d if self.backward else here["y"] + d

                @pl.when(to >= 0 if self.backward else to < 4)
                def _():
                    act(remote(self.along_y.at[here["y"]], self.along_y.at[here["y"]], self.s.at[2 + d],
                               self.r.at[3 + here["y"]], (to * 2 + x_low, dp)))

        def first(self):
            self.to_pair.start()
            pl.when(self.tells)(self.to_pair_rest.start)

        def second(self):
            self.to_pair.wait_recv()
            mine, theirs = self.own[my_half, :].astype(F32), self.other[my_half, :].astype(F32)
            near, away = jnp.where(self.tells, theirs, mine), jnp.where(self.tells, mine, theirs)
            self.along_y[here["y"]] = (shard_decay * away + near).astype(BF16)
            self.each_y(lambda copy: copy.start())

        def third(self):
            acc_ref[...] = jnp.zeros_like(acc_ref)

            def take(k, _):
                i = 3 - k if self.backward else k
                arrived(self.along_y.at[i], self.r.at[3 + i])
                acc_ref[...] = acc_ref[...] * pair_decay + self.along_y[i].astype(F32)
                return _

            lax.fori_loop(0, 3 - here["y"] if self.backward else here["y"], take, 0)
            self.total[my_half, :] = acc_ref[...].astype(BF16)
            self.halves.start()

        def result(self):
            self.halves.wait_recv()
            pl.when(self.hears)(self.to_pair_rest.wait_recv)
            total = self.total[...].astype(F32)
            return jnp.where(self.hears, shard_decay * total + self.other[...].astype(F32), total)

        def sent(self):
            self.to_pair.wait_send()
            pl.when(self.tells)(self.to_pair_rest.wait_send)
            self.each_y(lambda copy: copy.wait_send())
            self.halves.wait_send()

    states = Exchange(st, st_pair, st_y, st_sum, st_s, st_r, False)
    grad_states = Exchange(gs, gs_pair, gs_y, gs_sum, gs_s, gs_r, True)

    ag_done(0)
    ag_done(1)
    project(K)
    ks_ref[...] = (rotated(pr[K]) * twice(down_ref[...])).astype(BF16)
    ag_done(2)
    project(V)
    v_ref[...] = pr[V].astype(BF16)
    st[...] = (dot(v_ref[...], ks_ref[...], 0, 0) * jnp.exp(-(CENTER - 1.0) * rates)).astype(BF16)
    states.first()
    for n in QGO:
        ag_relay(n, 2)
    states.second()
    for n in QGO:
        ag_opposite(n)
    states.third()
    ag_done(3)
    project(Q)
    qs_ref[...] = (rotated(pr[Q]) * twice(up_ref[...])).astype(BF16)
    before = lax.broadcasted_iota(jnp.int32, (ROWS, ROWS), 0) >= lax.broadcasted_iota(jnp.int32, (ROWS, ROWS), 1)
    score_ref[...] = jnp.where(before, dot(qs_ref[...], ks_ref[...], 1, 1), 0.0).astype(BF16)
    ag_done(4)
    project(GATE)
    state = (states.result() * jnp.exp(-(CENTER + 1.0) * rates)).astype(BF16)
    retained = dot(score_ref[...], v_ref[...], 1, 0) + dot(qs_ref[...], state, 1, 1)
    inverse = lax.rsqrt(jnp.mean(retained * retained, axis=1, keepdims=True) + EPSILON)
    normed = retained * inverse

    ag_done(5)
    project(OUT)
    gate = pr[GATE].astype(BF16).astype(F32)
    grad_hidden = pr[OUT]
    sig = jax.nn.sigmoid(gate)
    hid_ref[...] = (gate * sig * normed).astype(BF16)
    grad_normed = grad_hidden * gate * sig
    gp[:, lanes_of(GATE)] = (grad_hidden * normed * sig * (1.0 + gate * (1.0 - sig))).astype(BF16)
    gret_ref[...] = (
        inverse * (grad_normed - normed * jnp.mean(grad_normed * normed, axis=1, keepdims=True))
    ).astype(BF16)

    gs[...] = (dot(gret_ref[...], qs_ref[...], 0, 0) * jnp.exp(-float(CENTER) * rates)).astype(BF16)
    grad_states.first()

    def half_term(g, c, of_core):
        left = ut if g == OUT else xt
        right = hid_ref[...] if g == OUT else gp[:, lanes_of(g)]
        return dot(left[pl.ds(2 * c, 2), :, :, :, of_core].reshape(1024, ROWS), right, 1, 0).reshape(2, 2, 4, 2, 2, 16, HEAD)

    def term(g):
        def step(c, _):
            pb[pl.ds(2 * c, 2), ..., lanes_of(g)] = half_term(g, c, 1 - core).astype(BF16)
            return _

        lax.fori_loop(0, 2, step, 0)
        lanes = pl.ds(g * HEAD, HEAD)
        at = (EVERY,) * 6 + (lanes,)
        send(pb.at[at], sb.at[at], sib_s.at[0], sib_r.at[g], sibling)

    def pair(g):
        arrived(sb.at[(EVERY,) * 6 + (pl.ds(g * HEAD, HEAD),)], sib_r.at[g])

        def step(c, _):
            at = (pl.ds(2 * c, 2),) + (EVERY,) * 5 + (lanes_of(g),)
            sb[at] = (half_term(g, c, core) + sb[at].astype(F32)).astype(BF16)
            return _

        lax.fori_loop(0, 2, step, 0)

    def s_idx(n, **fixed):
        rows, lanes, _ = PIECES[n]
        return place(**fixed) + (rows, EVERY, lanes)

    def rs_axis(n, k):
        a1, a2, a3 = ORDERS[n % 3]
        if k == 0:
            return a3, SPLIT[a3], {}, far_a[n], near_a[n]
        return a2, a1, {a3: here[a3]}, far_b[n], near_b[n]

    def half_of(n, k, side):
        axis, split, _, far, _ = rs_axis(n, k)
        half = pl.ds(side, 1) if split == "x" else pl.ds(2 * side, 2)
        return far.at[(EVERY, half) if split == "x" or (k == 0 and axis == "y") else (half,)]

    def rs_first(n, k):
        axis, split, fixed, _, _ = rs_axis(n, k)
        far = shifted(axis, 2)
        for side, by in ((0, 1), (1, 3)):
            src = sb.at[s_idx(n, half=(split, side), **{**fixed, axis: far})]
            send(src, half_of(n, k, side), rs_s.at[2 * k], rs_r.at[n, 2 * k], peer(axis, by))

    def rs_second(n, k):
        axis, split, fixed, far, near = rs_axis(n, k)
        arrived(far, rs_r.at[n, 2 * k])
        for side, by in ((0, 1), (1, 3)):
            at = s_idx(n, half=(split, side), **{**fixed, axis: shifted(axis, by)})
            sb[at] = (sb[at].astype(F32) + half_of(n, k, side)[...].astype(F32)).astype(BF16)
            send(sb.at[s_idx(n, **{**fixed, axis: shifted(axis, by)})], near.at[side],
                 rs_s.at[2 * k + 1], rs_r.at[n, 2 * k + 1], peer(axis, by))

    def rs_third(n, k):
        axis, _, fixed, _, near = rs_axis(n, k)
        arrived(near, rs_r.at[n, 2 * k + 1])
        at = s_idx(n, **{**fixed, axis: here[axis]})
        sb[at] = (sb[at].astype(F32) + near[0].astype(F32) + near[1].astype(F32)).astype(BF16)
        if k == 0:
            rs_first(n, 1)
            return
        a1 = ORDERS[n % 3][0]
        for k, by in enumerate((1, 3, 2)):
            src = sb.at[s_idx(n, **{**here, a1: shifted(a1, by)})]
            send(src, last[n].at[k], rs_s.at[4], rs_r.at[n, 4], peer(a1, by))

    def rs_end(n):
        rows, lanes, to = PIECES[n]
        arrived(last[n], rs_r.at[n, 4])
        total = sb[s_idx(n, **here)].astype(F32)
        for k in range(3):
            total += last[n][k].astype(F32)
        total = total.reshape(-1, total.shape[-1])
        out_rows = EVERY if rows == EVERY else slice(16 * rows, 16 * rows + 16)
        if to is None:
            gwout_ref[out_rows, :] = total
        else:
            gwin_ref[out_rows, slice(to, to + total.shape[-1])] = total

    puts = []

    def grad_input(c):
        slot = c % 2
        if c >= 2:
            puts[c - 2].wait()
        stage[slot] = dot(gp[...], wg[c, ..., slice(0, 4 * HEAD)].reshape(1024, 4 * HEAD), 1, 1).astype(BF16)
        put = pltpu.make_async_copy(stage.at[slot], gin_hbm.at[:, pl.ds(c * 1024, 1024)], out_sem.at[slot])
        put.start()
        puts.append(put)

    term(OUT)
    term(GATE)
    grad_states.second()
    score_grad = jnp.where(before, dot(gret_ref[...], v_ref[...], 1, 1), 0.0).astype(BF16)
    grad_q = dot(score_grad, ks_ref[...], 1, 0) + dot(gret_ref[...], state, 1, 0)
    gp[:, lanes_of(Q)] = unrotated(grad_q * twice(up_ref[...]))
    term(Q)
    pair(OUT)
    rs_first(5, 0)
    pair(GATE)
    rs_first(4, 0)
    grad_states.third()
    pair(Q)
    rs_first(3, 0)
    grad_k = dot(score_grad, qs_ref[...], 0, 0)
    rs_second(5, 0)
    rs_second(4, 0)
    grad_state = (grad_states.result() * jnp.exp(-float(CENTER) * rates)).astype(BF16)
    gp[:, lanes_of(K)] = unrotated((grad_k + dot(v_ref[...], grad_state, 1, 0)) * twice(down_ref[...]))
    term(K)
    rs_second(3, 0)
    grad_v = dot(score_ref[...], gret_ref[...], 0, 0) + dot(ks_ref[...], grad_state, 1, 1)
    gp[:, lanes_of(V)] = grad_v.astype(BF16)
    term(V)
    pair(K)
    pair(V)
    for n in KV:
        rs_first(n, 0)
    grad_input(0)
    for n in (5, 4, 3):
        rs_third(n, 0)
    grad_input(1)
    for n in KV:
        rs_second(n, 0)
    for n in (5, 4, 3):
        rs_second(n, 1)
    grad_input(2)
    for n in (5, 4, 3):
        rs_third(n, 1)
    for n in KV:
        rs_third(n, 0)
    grad_input(3)
    for n in KV:
        rs_second(n, 1)
    for n in (5, 4, 3):
        rs_end(n)
    for n in KV:
        rs_third(n, 1)
    for n in KV:
        rs_end(n)
    for put in puts[2:]:
        put.wait()
    for step, of in enumerate(W_BYTES):
        sent(wg.at[of + (0,)], ag_s.at[step])
    sent(sb, sib_s.at[0])
    for step, of in enumerate(((0,), (slice(0, 2),), (slice(0, 1), 0, EVERY, 0), (slice(0, 2), 0, EVERY, 0), (slice(0, 3), 0, 0, 0))):
        sent(sb.at[of], rs_s.at[step])
    states.sent()
    grad_states.sent()


def publish(a, b, c, a_out, b_out, c_out, sem):
    copies = [pltpu.make_async_copy(b, b_out, sem.at[0]), pltpu.make_async_copy(c, c_out, sem.at[1])]
    for k in range(4):
        rows = pl.ds(k * ROWS // 4, ROWS // 4)
        copies.append(pltpu.make_async_copy(a.at[rows], a_out.at[rows], sem.at[2 + k]))
    for copy in copies:
        copy.start()
    for copy in copies:
        copy.wait()


def on_device(layer_input, grad_out, w_in, w_out_t, decay_rate):
    hbm, vmem = pl.BlockSpec(memory_space=pl.ANY), pl.BlockSpec(memory_space=pltpu.VMEM)
    dma = pltpu.SemaphoreType.DMA
    buf = pltpu.VMEM
    axis_of = [ORDERS[n % 3][2] for n in range(6)]
    results = (
        jax.ShapeDtypeStruct((ROWS, WIDTH), BF16),
        jax.ShapeDtypeStruct((32, 4 * HEAD), F32),
        jax.ShapeDtypeStruct((32, HEAD), F32),
    )
    held = pl.pallas_call(
        body,
        out_shape=results,
        in_specs=[hbm, hbm, hbm, hbm, vmem],
        out_specs=(hbm, vmem, vmem),
        scratch_shapes=[
            buf((ROWS, WIDTH), BF16),
            buf((ROWS, WIDTH), BF16),
            buf((4, 2, 4, 2, 2, 32, ROWS), BF16),
            buf((4, 2, 4, 2, 2, 32, ROWS), BF16),
            buf((4, 2, 4, 2, 2, 2, 16, 5 * HEAD), BF16),
            buf((5, ROWS, HEAD), F32),
            buf((4, 2, 4, 2, 2, 16, 5 * HEAD), BF16),
            buf((4, 2, 4, 2, 2, 16, 5 * HEAD), BF16),
            buf((ROWS, 4 * HEAD), BF16),
            buf((ROWS, HALF), F32), buf((ROWS, HALF), F32), buf((ROWS, HALF), F32), buf((ROWS, HALF), F32),
            buf((ROWS, HEAD), BF16), buf((ROWS, HEAD), BF16), buf((ROWS, HEAD), BF16),
            buf((ROWS, ROWS), BF16),
            buf((HEAD // 2, HEAD), F32),
            *[buf(dims, BF16) for dims in ((HEAD, HEAD), (HEAD, HEAD), (4, HEAD // 2, HEAD), (HEAD, HEAD)) * 2],
            buf((ROWS, HEAD), BF16), buf((ROWS, HEAD), BF16),
            buf((2, ROWS, 1024), BF16),
            *[buf(BLOCK_DIMS[axis_of[n]] + inner(n), BF16) for n in range(6)],
            *[buf((2,) + BLOCK_DIMS[axis_of[n]] + inner(n), BF16) for n in range(6)],
            *[buf(PART_DIMS[axis_of[n]] + inner(n), BF16) for n in range(6)],
            *[buf((2,) + PART_DIMS[axis_of[n]] + inner(n), BF16) for n in range(6)],
            *[buf((3,) + inner(n), BF16) for n in range(6)],
            dma((6,)), dma((6, 6)),
            dma((6,)), dma((7,)), dma((6,)), dma((7,)),
            dma((1,)), dma((5,)),
            dma((5,)), dma((6, 5)),
            dma((3,)), dma((2,)),
        ],
        compiler_params=pltpu.CompilerParams(
            collective_id=0, has_side_effects=True, vmem_limit_bytes=62 * 1024 * 1024
        ),
        cost_estimate=pl.CostEstimate(flops=17 * 10**9, bytes_accessed=13 * 10**6, transcendentals=10**6),
        name="retention_backward",
    )(layer_input[0], grad_out[0], w_in.reshape(2, 16, 4 * HEAD), w_out_t.reshape(2, 16, HEAD), decay_rate[None, :])
    grad_in, grad_w, grad_wo = pl.pallas_call(
        publish, out_shape=results, in_specs=[hbm] * 3, out_specs=(hbm,) * 3, scratch_shapes=[dma((6,))], name="publish",
    )(*held)
    return grad_in[None], grad_w, grad_wo


def solution(mesh):
    rows = P(("ctx", "dp"), None)
    tokens = P("dp", "ctx", None)
    return jax.shard_map(
        on_device,
        mesh=mesh,
        in_specs=(tokens, tokens, rows, rows, P()),
        out_specs=(tokens, rows, rows),
        check_vma=False,
    )
```

```python
import math

import jax
import jax.numpy as jnp
from jax import lax
from jax.experimental import pallas as pl
from jax.experimental.pallas import tpu as pltpu
from jax.sharding import PartitionSpec as P

EPSILON = 1e-06
MESH = pl.DeviceIdType.MESH
F32, BF16 = jnp.float32, jnp.bfloat16
ROWS, WIDTH, HEAD, HALF = 512, 4096, 256, 128
CENTER = ROWS // 2
K, V, Q, GATE, OUT = range(5)
EVERY = slice(None)
ORDERS = (("x", "y", "z"), ("y", "z", "x"), ("z", "x", "y"))
PIECES = (
    (0, slice(0, 384), 256), (1, slice(0, 384), 256), (EVERY, slice(384, 512), 640),
    (EVERY, slice(512, 768), 0), (EVERY, slice(768, 1024), 768), (EVERY, slice(1024, 1280), None),
)
KV, QGO = (0, 1, 2), (3, 4, 5)
SPLIT = {"x": "y", "y": "z", "z": "y"}
BLOCK_DIMS = {"x": (4, 4), "y": (2, 4, 2), "z": (4, 2, 2)}
PART_DIMS = {"x": (4,), "y": (4,), "z": (2, 2)}


def inner(n):
    rows, lanes, _ = PIECES[n]
    return ((2,) if rows == EVERY else ()) + (16, lanes.stop - lanes.start)


def lanes_of(g):
    return slice(g * HEAD, (g + 1) * HEAD)


def dot(a, b, ca, cb):
    return lax.dot_general(a, b, (((ca,), (cb,)), ((), ())), preferred_element_type=F32)


def place(half=None, x=None, y=None, z=None):
    where = {"y": EVERY if y is None else y, "z": EVERY if z is None else z}
    if half is not None and half[0] != "x":
        where[half[0]] = pl.ds(2 * half[1], 2)
    if x is None:
        return (where["y"], EVERY, where["z"], pl.ds(half[1], 1) if half is not None and half[0] == "x" else EVERY)
    return (where["y"], lax.rem(x, 2), where["z"], lax.div(x, 2))


def body(x_hbm, u_hbm, win_hbm, wout_hbm, rate_ref, gin_hbm, gwin_ref, gwout_ref,
         xv, uv, xt, ut, wg, pr, pb, sb, gp, cos_ref, sin_ref, up_ref, down_ref, qs_ref, ks_ref, v_ref, score_ref, acc_ref,
         st, st_pair, st_y, st_sum, gs, gs_pair, gs_y, gs_sum, hid_ref, gret_ref, stage, *rest):
    far_a, near_a, far_b, near_b, last = (rest[6 * k:6 * k + 6] for k in range(5))
    ag_s, ag_r, st_s, st_r, gs_s, gs_r, sib_s, sib_r, rs_s, rs_r, load_sem, out_sem = rest[30:]
    ctx, dp = lax.axis_index("ctx"), lax.axis_index("dp")
    core = lax.rem(dp, 2)
    here = {
        "x": lax.rem(lax.div(dp, 2), 2) * 2 + lax.rem(ctx, 2),
        "y": lax.div(ctx, 2),
        "z": lax.div(dp, 4),
    }

    def device(at, on_core):
        return (at["y"] * 2 + lax.rem(at["x"], 2), at["z"] * 4 + lax.div(at["x"], 2) * 2 + on_core)

    def shifted(axis, by):
        return lax.rem(here[axis] + by, 4)

    def peer(axis, by):
        return device({**here, axis: shifted(axis, by)}, core)

    sibling = (ctx, dp + 1 - 2 * core)

    def remote(src, dst, send, recv, to):
        return pltpu.make_async_remote_copy(
            src_ref=src, dst_ref=dst, send_sem=send, recv_sem=recv, device_id=to, device_id_type=MESH
        )

    mine = place(**here) + (core,)
    own = wg.at[mine]
    for src, first, to, size in ((win_hbm, HEAD, K, 2), (win_hbm, 0, Q, 1), (win_hbm, 3 * HEAD, GATE, 1), (wout_hbm, 0, OUT, 1)):
        src = src.at[:, :, pl.ds(first, size * HEAD)]
        pltpu.make_async_copy(src, wg.at[mine + (EVERY, EVERY, pl.ds(to * HEAD, size * HEAD))], load_sem.at[2]).start()
    load_x = pltpu.make_async_copy(x_hbm, xv, load_sem.at[0])
    load_u = pltpu.make_async_copy(u_hbm, uv, load_sem.at[1])
    load_x.start()
    load_u.start()

    greeted = [peer(axis, by) for axis in "xyz" for by in (1, 2, 3)] + [sibling]
    barrier = pltpu.get_barrier_semaphore()
    for to in greeted:
        pl.semaphore_signal(barrier, inc=1, device_id=to, device_id_type=MESH)
    pl.semaphore_wait(barrier, len(greeted))

    def send(src, dst, send_sem, recv_sem, to):
        remote(src, dst, send_sem, recv_sem, to).start()

    def arrived(ref, recv_sem):
        remote(ref, ref, ag_s.at[0], recv_sem, sibling).wait_recv()

    def sent(ref, send_sem):
        remote(ref, ref, send_sem, ag_r.at[0, 0], sibling).wait_send()

    def w_at(n, **fixed):
        rows, lanes, _ = PIECES[n]
        return wg.at[place(**fixed) + (core, rows, EVERY, lanes)]

    W_BYTES = ((slice(0, 3), 0, 0, 0), (slice(0, 2), 0, EVERY, 0), (slice(0, 1), 0, EVERY, 0),
               (slice(0, 2), EVERY, EVERY, EVERY), (0, EVERY, EVERY, EVERY), (EVERY, EVERY, EVERY, EVERY))

    def ag_send(n, step, to, **fixed):
        send(w_at(n, **fixed), w_at(n, **fixed), ag_s.at[step], ag_r.at[n, step], to)

    def ag_wait(n, step):
        rows, lanes, _ = PIECES[n]
        arrived(wg.at[W_BYTES[step] + (0, rows, EVERY, lanes)], ag_r.at[n, step])

    def ag_first(n):
        axis = ORDERS[n % 3][0]
        for by in (1, 3, 2):
            ag_send(n, 0, peer(axis, by), **here)

    def ag_both(n, k):
        order = ORDERS[n % 3]
        axis, fixed = order[k], {a: here[a] for a in order[k:]}
        for by in (1, 3):
            ag_send(n, 2 * k - 1, peer(axis, by), **fixed)
        if k == 2:
            ag_send(n, 5, sibling, **fixed)

    def ag_relay(n, k):
        order = ORDERS[n % 3]
        axis, fixed = order[k], {a: here[a] for a in order[k:]}
        split = order[0] if k == 1 else SPLIT[axis]
        ag_wait(n, 2 * k - 1)
        for by, side in ((1, 0), (3, 1)):
            ag_send(n, 2 * k, peer(axis, by), half=(split, side), **{**fixed, axis: shifted(axis, 4 - by)})
        if k == 2:
            for by in (1, 3):
                ag_send(n, 5, sibling, **{**fixed, axis: shifted(axis, by)})

    def ag_opposite(n):
        axis = ORDERS[n % 3][2]
        ag_wait(n, 4)
        ag_send(n, 5, sibling, **{axis: shifted(axis, 2)})

    def ag_done(n):
        ag_wait(n, 5)

    pltpu.make_async_copy(own, own, load_sem.at[2]).wait()
    for n in KV + QGO:
        ag_first(n)

    rate = rate_ref[...]
    row = lax.broadcasted_iota(jnp.int32, (ROWS, HALF), 0).astype(F32)
    spacing = jnp.exp(
        lax.broadcasted_iota(jnp.int32, (1, HALF), 1).astype(F32) * (-math.log(10000.0) / HALF)
    )

    def make_tables():
        angle = (row + (ctx * ROWS).astype(F32)) * spacing
        cos_ref[...] = jnp.cos(angle)
        sin_ref[...] = jnp.sin(angle)
        up_ref[...] = jnp.exp((CENTER - row) * rate)
        down_ref[...] = jnp.exp((row - CENTER) * rate)

    rates = jnp.concatenate([rate, rate], axis=1)

    def transpose(src, dst):
        def step(c, _):
            at = pl.ds(pl.multiple_of(c * 512, 512), 512)
            dst[lax.div(c, 2), lax.rem(c, 2)] = src[:, at].T.reshape(4, 2, 2, 32, ROWS)
            return _
        lax.fori_loop(0, 8, step, 0)

    make_tables()
    for n in KV:
        ag_wait(n, 0)
        ag_both(n, 1)
    for n in KV:
        ag_relay(n, 1)
    for n in QGO:
        ag_wait(n, 0)
        ag_both(n, 1)
    for n in KV:
        ag_wait(n, 2)
        ag_both(n, 2)
    for n in QGO:
        ag_relay(n, 1)
    load_x.wait()
    transpose(xv, xt)
    for n in KV:
        ag_relay(n, 2)
    for n in QGO:
        ag_wait(n, 2)
        ag_both(n, 2)
    load_u.wait()
    transpose(uv, ut)
    for n in KV:
        ag_opposite(n)

    def project(g):
        left = uv if g == OUT else xv
        pr[g] = dot(left[...], wg[..., lanes_of(g)].reshape(WIDTH, HEAD), 1, 0)

    def rotated(a):
        a = a.astype(BF16).astype(F32)
        a1, a2 = a[:, :HALF], a[:, HALF:]
        cos, sin = cos_ref[...], sin_ref[...]
        return jnp.concatenate([a1 * cos - a2 * sin, a1 * sin + a2 * cos], axis=1).astype(BF16).astype(F32)

    def unrotated(g):
        g1, g2 = g[:, :HALF], g[:, HALF:]
        cos, sin = cos_ref[...], sin_ref[...]
        return jnp.concatenate([g1 * cos + g2 * sin, g2 * cos - g1 * sin], axis=1).astype(BF16)

    def twice(t):
        return jnp.concatenate([t, t], axis=1)

    x_low = lax.rem(ctx, 2)
    pair_at = (ctx + 1 - 2 * x_low, dp)
    my_half, pair_half = pl.ds(128 * x_low, 128), pl.ds(128 * (1 - x_low), 128)
    shard_decay = jnp.exp(-float(ROWS) * rates)
    pair_decay = jnp.exp(-2.0 * ROWS * rates)

    class Exchange:
        def __init__(self, own, other, along_y, total, send_sem, recv_sem, backward):
            self.own, self.other, self.along_y, self.total = own, other, along_y, total
            self.s, self.r = send_sem, recv_sem
            self.hears, self.tells = (x_low == 0, x_low == 1) if backward else (x_low == 1, x_low == 0)
            self.backward = backward
            self.to_pair = remote(own.at[pair_half], other.at[pair_half], self.s.at[0], self.r.at[0], pair_at)
            self.to_pair_rest = remote(own.at[my_half], other.at[my_half], self.s.at[1], self.r.at[1], pair_at)
            self.halves = remote(total.at[my_half], total.at[my_half], self.s.at[2], self.r.at[2], pair_at)

        def each_y(self, act):
            for d in range(1, 4):
                to = here["y"] - d if self.backward else here["y"] + d

                @pl.when(to >= 0 if self.backward else to < 4)
                def _():
                    act(remote(self.along_y.at[here["y"]], self.along_y.at[here["y"]], self.s.at[2 + d],
                               self.r.at[3 + here["y"]], (to * 2 + x_low, dp)))

        def first(self):
            self.to_pair.start()
            pl.when(self.tells)(self.to_pair_rest.start)

        def second(self):
            self.to_pair.wait_recv()
            mine, theirs = self.own[my_half, :].astype(F32), self.other[my_half, :].astype(F32)
            near, away = jnp.where(self.tells, theirs, mine), jnp.where(self.tells, mine, theirs)
            self.along_y[here["y"]] = (shard_decay * away + near).astype(BF16)
            self.each_y(lambda copy: copy.start())

        def third(self):
            acc_ref[...] = jnp.zeros_like(acc_ref)

            def take(k, _):
                i = 3 - k if self.backward else k
                arrived(self.along_y.at[i], self.r.at[3 + i])
                acc_ref[...] = acc_ref[...] * pair_decay + self.along_y[i].astype(F32)
                return _

            lax.fori_loop(0, 3 - here["y"] if self.backward else here["y"], take, 0)
            self.total[my_half, :] = acc_ref[...].astype(BF16)
            self.halves.start()

        def result(self):
            self.halves.wait_recv()
            pl.when(self.hears)(self.to_pair_rest.wait_recv)
            total = self.total[...].astype(F32)
            return jnp.where(self.hears, shard_decay * total + self.other[...].astype(F32), total)

        def sent(self):
            self.to_pair.wait_send()
            pl.when(self.tells)(self.to_pair_rest.wait_send)
            self.each_y(lambda copy: copy.wait_send())
            self.halves.wait_send()

    states = Exchange(st, st_pair, st_y, st_sum, st_s, st_r, False)
    grad_states = Exchange(gs, gs_pair, gs_y, gs_sum, gs_s, gs_r, True)

    ag_done(0)
    ag_done(1)
    project(K)
    ks_ref[...] = (rotated(pr[K]) * twice(down_ref[...])).astype(BF16)
    ag_done(2)
    project(V)
    v_ref[...] = pr[V].astype(BF16)
    st[...] = (dot(v_ref[...], ks_ref[...], 0, 0) * jnp.exp(-(CENTER - 1.0) * rates)).astype(BF16)
    states.first()
    for n in QGO:
        ag_relay(n, 2)
    states.second()
    for n in QGO:
        ag_opposite(n)
    states.third()
    ag_done(3)
    project(Q)
    qs_ref[...] = (rotated(pr[Q]) * twice(up_ref[...])).astype(BF16)
    before = lax.broadcasted_iota(jnp.int32, (ROWS, ROWS), 0) >= lax.broadcasted_iota(jnp.int32, (ROWS, ROWS), 1)
    score_ref[...] = jnp.where(before, dot(qs_ref[...], ks_ref[...], 1, 1), 0.0).astype(BF16)
    ag_done(4)
    project(GATE)
    state = (states.result() * jnp.exp(-(CENTER + 1.0) * rates)).astype(BF16)
    retained = dot(score_ref[...], v_ref[...], 1, 0) + dot(qs_ref[...], state, 1, 1)
    inverse = lax.rsqrt(jnp.mean(retained * retained, axis=1, keepdims=True) + EPSILON)
    normed = retained * inverse

    ag_done(5)
    project(OUT)
    gate = pr[GATE].astype(BF16).astype(F32)
    grad_hidden = pr[OUT]
    sig = jax.nn.sigmoid(gate)
    hid_ref[...] = (gate * sig * normed).astype(BF16)
    grad_normed = grad_hidden * gate * sig
    gp[:, lanes_of(GATE)] = (grad_hidden * normed * sig * (1.0 + gate * (1.0 - sig))).astype(BF16)
    gret_ref[...] = (
        inverse * (grad_normed - normed * jnp.mean(grad_normed * normed, axis=1, keepdims=True))
    ).astype(BF16)

    gs[...] = (dot(gret_ref[...], qs_ref[...], 0, 0) * jnp.exp(-float(CENTER) * rates)).astype(BF16)
    grad_states.first()

    def half_term(g, c, of_core):
        left = ut if g == OUT else xt
        right = hid_ref[...] if g == OUT else gp[:, lanes_of(g)]
        return dot(left[pl.ds(2 * c, 2), :, :, :, of_core].reshape(1024, ROWS), right, 1, 0).reshape(2, 2, 4, 2, 2, 16, HEAD)

    def term(g):
        def step(c, _):
            pb[pl.ds(2 * c, 2), ..., lanes_of(g)] = half_term(g, c, 1 - core).astype(BF16)
            return _

        lax.fori_loop(0, 2, step, 0)
        lanes = pl.ds(g * HEAD, HEAD)
        at = (EVERY,) * 6 + (lanes,)
        send(pb.at[at], sb.at[at], sib_s.at[0], sib_r.at[g], sibling)

    def pair(g):
        arrived(sb.at[(EVERY,) * 6 + (pl.ds(g * HEAD, HEAD),)], sib_r.at[g])

        def step(c, _):
            at = (pl.ds(2 * c, 2),) + (EVERY,) * 5 + (lanes_of(g),)
            sb[at] = (half_term(g, c, core) + sb[at].astype(F32)).astype(BF16)
            return _

        lax.fori_loop(0, 2, step, 0)

    def s_idx(n, **fixed):
        rows, lanes, _ = PIECES[n]
        return place(**fixed) + (rows, EVERY, lanes)

    def rs_axis(n, k):
        a1, a2, a3 = ORDERS[n % 3]
        if k == 0:
            return a3, SPLIT[a3], {}, far_a[n], near_a[n]
        return a2, a1, {a3: here[a3]}, far_b[n], near_b[n]

    def half_of(n, k, side):
        axis, split, _, far, _ = rs_axis(n, k)
        half = pl.ds(side, 1) if split == "x" else pl.ds(2 * side, 2)
        return far.at[(EVERY, half) if split == "x" or (k == 0 and axis == "y") else (half,)]

    def rs_first(n, k):
        axis, split, fixed, _, _ = rs_axis(n, k)
        far = shifted(axis, 2)
        for side, by in ((0, 1), (1, 3)):
            src = sb.at[s_idx(n, half=(split, side), **{**fixed, axis: far})]
            send(src, half_of(n, k, side), rs_s.at[2 * k], rs_r.at[n, 2 * k], peer(axis, by))

    def rs_second(n, k):
        axis, split, fixed, far, near = rs_axis(n, k)
        arrived(far, rs_r.at[n, 2 * k])
        for side, by in ((0, 1), (1, 3)):
            at = s_idx(n, half=(split, side), **{**fixed, axis: shifted(axis, by)})
            sb[at] = (sb[at].astype(F32) + half_of(n, k, side)[...].astype(F32)).astype(BF16)
            send(sb.at[s_idx(n, **{**fixed, axis: shifted(axis, by)})], near.at[side],
                 rs_s.at[2 * k + 1], rs_r.at[n, 2 * k + 1], peer(axis, by))

    def rs_third(n, k):
        axis, _, fixed, _, near = rs_axis(n, k)
        arrived(near, rs_r.at[n, 2 * k + 1])
        at = s_idx(n, **{**fixed, axis: here[axis]})
        sb[at] = (sb[at].astype(F32) + near[0].astype(F32) + near[1].astype(F32)).astype(BF16)
        if k == 0:
            rs_first(n, 1)
            return
        a1 = ORDERS[n % 3][0]
        for k, by in enumerate((1, 3, 2)):
            src = sb.at[s_idx(n, **{**here, a1: shifted(a1, by)})]
            send(src, last[n].at[k], rs_s.at[4], rs_r.at[n, 4], peer(a1, by))

    def rs_end(n):
        rows, lanes, to = PIECES[n]
        arrived(last[n], rs_r.at[n, 4])
        total = sb[s_idx(n, **here)].astype(F32)
        for k in range(3):
            total += last[n][k].astype(F32)
        total = total.reshape(-1, total.shape[-1])
        out_rows = EVERY if rows == EVERY else slice(16 * rows, 16 * rows + 16)
        if to is None:
            gwout_ref[out_rows, :] = total
        else:
            gwin_ref[out_rows, slice(to, to + total.shape[-1])] = total

    puts = []

    def grad_input(c):
        slot = c % 2
        if c >= 2:
            puts[c - 2].wait()
        stage[slot] = dot(gp[...], wg[c, ..., slice(0, 4 * HEAD)].reshape(1024, 4 * HEAD), 1, 1).astype(BF16)
        put = pltpu.make_async_copy(stage.at[slot], gin_hbm.at[:, pl.ds(c * 1024, 1024)], out_sem.at[slot])
        put.start()
        puts.append(put)

    term(OUT)
    grad_states.second()
    term(GATE)
    score_grad = jnp.where(before, dot(gret_ref[...], v_ref[...], 1, 1), 0.0).astype(BF16)
    grad_states.third()
    pair(OUT)
    rs_first(5, 0)
    grad_q = dot(score_grad, ks_ref[...], 1, 0) + dot(gret_ref[...], state, 1, 0)
    gp[:, lanes_of(Q)] = unrotated(grad_q * twice(up_ref[...]))
    term(Q)
    pair(GATE)
    rs_first(4, 0)
    pr[K] = dot(score_grad, qs_ref[...], 0, 0)
    pr[V] = dot(score_ref[...], gret_ref[...], 0, 0)
    grad_state = (grad_states.result() * jnp.exp(-float(CENTER) * rates)).astype(BF16)
    gp[:, lanes_of(K)] = unrotated((pr[K] + dot(v_ref[...], grad_state, 1, 0)) * twice(down_ref[...]))
    gp[:, lanes_of(V)] = (pr[V] + dot(ks_ref[...], grad_state, 1, 1)).astype(BF16)
    term(K)
    pair(Q)
    rs_first(3, 0)
    term(V)
    rs_second(5, 0)
    rs_second(4, 0)
    pair(K)
    rs_second(3, 0)
    pair(V)
    for n in KV:
        rs_first(n, 0)
    for n in (5, 4, 3):
        rs_third(n, 0)
    grad_input(0)
    for n in KV:
        rs_second(n, 0)
    for n in (5, 4, 3):
        rs_second(n, 1)
    grad_input(1)
    for n in (5, 4, 3):
        rs_third(n, 1)
    grad_input(2)
    for n in KV:
        rs_third(n, 0)
    grad_input(3)
    for n in KV:
        rs_second(n, 1)
    for n in (5, 4, 3):
        rs_end(n)
    for n in KV:
        rs_third(n, 1)
    for n in KV:
        rs_end(n)
    for put in puts[2:]:
        put.wait()
    for step, of in enumerate(W_BYTES):
        sent(wg.at[of + (0,)], ag_s.at[step])
    sent(sb, sib_s.at[0])
    for step, of in enumerate(((0,), (slice(0, 2),), (slice(0, 1), 0, EVERY, 0), (slice(0, 2), 0, EVERY, 0), (slice(0, 3), 0, 0, 0))):
        sent(sb.at[of], rs_s.at[step])
    states.sent()
    grad_states.sent()


def publish(a, b, c, a_out, b_out, c_out, a_held, b_held, c_held, in_sem, out_sem):
    ways = [(b, b_held, b_out), (c, c_held, c_out)]
    for k in range(4):
        rows = pl.ds(k * ROWS // 4, ROWS // 4)
        ways.append((a.at[rows], a_held.at[rows], a_out.at[rows]))
    loads = [pltpu.make_async_copy(src, held, in_sem.at[k]) for k, (src, held, _) in enumerate(ways)]
    stores = [pltpu.make_async_copy(held, dst, out_sem.at[k]) for k, (_, held, dst) in enumerate(ways)]
    for load in loads:
        load.start()
    for load, store in zip(loads, stores):
        load.wait()
        store.start()
    for store in stores:
        store.wait()


def on_device(layer_input, grad_out, w_in, w_out_t, decay_rate):
    hbm, vmem = pl.BlockSpec(memory_space=pl.ANY), pl.BlockSpec(memory_space=pltpu.VMEM)
    dma = pltpu.SemaphoreType.DMA
    buf = pltpu.VMEM
    axis_of = [ORDERS[n % 3][2] for n in range(6)]
    results = (
        jax.ShapeDtypeStruct((ROWS, WIDTH), BF16),
        jax.ShapeDtypeStruct((32, 4 * HEAD), F32),
        jax.ShapeDtypeStruct((32, HEAD), F32),
    )
    held = pl.pallas_call(
        body,
        out_shape=results,
        in_specs=[hbm, hbm, hbm, hbm, vmem],
        out_specs=(hbm, vmem, vmem),
        scratch_shapes=[
            buf((ROWS, WIDTH), BF16),
            buf((ROWS, WIDTH), BF16),
            buf((4, 2, 4, 2, 2, 32, ROWS), BF16),
            buf((4, 2, 4, 2, 2, 32, ROWS), BF16),
            buf((4, 2, 4, 2, 2, 2, 16, 5 * HEAD), BF16),
            buf((5, ROWS, HEAD), F32),
            buf((4, 2, 4, 2, 2, 16, 5 * HEAD), BF16),
            buf((4, 2, 4, 2, 2, 16, 5 * HEAD), BF16),
            buf((ROWS, 4 * HEAD), BF16),
            buf((ROWS, HALF), F32), buf((ROWS, HALF), F32), buf((ROWS, HALF), F32), buf((ROWS, HALF), F32),
            buf((ROWS, HEAD), BF16), buf((ROWS, HEAD), BF16), buf((ROWS, HEAD), BF16),
            buf((ROWS, ROWS), BF16),
            buf((HEAD // 2, HEAD), F32),
            *[buf(dims, BF16) for dims in ((HEAD, HEAD), (HEAD, HEAD), (4, HEAD // 2, HEAD), (HEAD, HEAD)) * 2],
            buf((ROWS, HEAD), BF16), buf((ROWS, HEAD), BF16),
            buf((2, ROWS, 1024), BF16),
            *[buf(BLOCK_DIMS[axis_of[n]] + inner(n), BF16) for n in range(6)],
            *[buf((2,) + BLOCK_DIMS[axis_of[n]] + inner(n), BF16) for n in range(6)],
            *[buf(PART_DIMS[axis_of[n]] + inner(n), BF16) for n in range(6)],
            *[buf((2,) + PART_DIMS[axis_of[n]] + inner(n), BF16) for n in range(6)],
            *[buf((3,) + inner(n), BF16) for n in range(6)],
            dma((6,)), dma((6, 6)),
            dma((6,)), dma((7,)), dma((6,)), dma((7,)),
            dma((1,)), dma((5,)),
            dma((5,)), dma((6, 5)),
            dma((3,)), dma((2,)),
        ],
        compiler_params=pltpu.CompilerParams(
            collective_id=0, has_side_effects=True, vmem_limit_bytes=62 * 1024 * 1024
        ),
        cost_estimate=pl.CostEstimate(flops=17 * 10**9, bytes_accessed=13 * 10**6, transcendentals=10**6),
        name="retention_backward",
    )(layer_input[0], grad_out[0], w_in.reshape(2, 16, 4 * HEAD), w_out_t.reshape(2, 16, HEAD), decay_rate[None, :])
    grad_in, grad_w, grad_wo = pl.pallas_call(
        publish, out_shape=results, in_specs=[hbm] * 3, out_specs=(hbm,) * 3, scratch_shapes=[*[buf(r.shape, r.dtype) for r in results], dma((6,)), dma((6,))], name="publish",
    )(*held)
    return grad_in[None], grad_w, grad_wo


def solution(mesh):
    rows = P(("ctx", "dp"), None)
    tokens = P("dp", "ctx", None)
    return jax.shard_map(
        on_device,
        mesh=mesh,
        in_specs=(tokens, tokens, rows, rows, P()),
        out_specs=(tokens, rows, rows),
        check_vma=False,
    )
```

```python
import math

import jax
import jax.numpy as jnp
from jax import lax
from jax.experimental import pallas as pl
from jax.experimental.pallas import tpu as pltpu
from jax.sharding import PartitionSpec as P

EPSILON = 1e-06
MESH = pl.DeviceIdType.MESH
F32, BF16 = jnp.float32, jnp.bfloat16
ROWS, WIDTH, HEAD, HALF = 512, 4096, 256, 128
CENTER = ROWS // 2
K, V, Q, GATE, OUT = range(5)
EVERY = slice(None)
ORDERS = (("x", "y", "z"), ("y", "z", "x"), ("z", "x", "y"))
PIECES = (
    (0, slice(0, 384), 256), (1, slice(0, 384), 256), (EVERY, slice(384, 512), 640),
    (EVERY, slice(512, 768), 0), (EVERY, slice(768, 1024), 768), (EVERY, slice(1024, 1280), None),
)
KV, QGO = (0, 1, 2), (3, 4, 5)
DIRECT = (1,)
DIRECT_BACK = (1,)
SPLIT = {"x": "y", "y": "z", "z": "y"}
BLOCK_DIMS = {"x": (4, 4), "y": (2, 4, 2), "z": (4, 2, 2)}
PART_DIMS = {"x": (4,), "y": (4,), "z": (2, 2)}


def inner(n):
    rows, lanes, _ = PIECES[n]
    return ((2,) if rows == EVERY else ()) + (16, lanes.stop - lanes.start)


def lanes_of(g):
    return slice(g * HEAD, (g + 1) * HEAD)


def dot(a, b, ca, cb):
    return lax.dot_general(a, b, (((ca,), (cb,)), ((), ())), preferred_element_type=F32)


def place(half=None, x=None, y=None, z=None):
    where = {"y": EVERY if y is None else y, "z": EVERY if z is None else z}
    if half is not None and half[0] != "x":
        where[half[0]] = pl.ds(2 * half[1], 2)
    if x is None:
        return (where["y"], EVERY, where["z"], pl.ds(half[1], 1) if half is not None and half[0] == "x" else EVERY)
    return (where["y"], lax.rem(x, 2), where["z"], lax.div(x, 2))


def body(x_hbm, u_hbm, win_hbm, wout_hbm, rate_ref, gin_hbm, gwin_ref, gwout_ref,
         xv, uv, xt, ut, wg, pr, pb, sb, gp, cos_ref, sin_ref, up_ref, down_ref, qs_ref, ks_ref, v_ref, score_ref, acc_ref,
         st, st_pair, st_y, st_sum, gs, gs_pair, gs_y, gs_sum, hid_ref, gret_ref, stage, *rest):
    far_a, near_a, far_b, near_b, last = (rest[6 * k:6 * k + 6] for k in range(5))
    ag_s, ag_r, st_s, st_r, gs_s, gs_r, sib_s, sib_r, rs_s, rs_r, load_sem, out_sem = rest[30:]
    ctx, dp = lax.axis_index("ctx"), lax.axis_index("dp")
    core = lax.rem(dp, 2)
    here = {
        "x": lax.rem(lax.div(dp, 2), 2) * 2 + lax.rem(ctx, 2),
        "y": lax.div(ctx, 2),
        "z": lax.div(dp, 4),
    }

    def device(at, on_core):
        return (at["y"] * 2 + lax.rem(at["x"], 2), at["z"] * 4 + lax.div(at["x"], 2) * 2 + on_core)

    def shifted(axis, by):
        return lax.rem(here[axis] + by, 4)

    def peer(axis, by):
        return device({**here, axis: shifted(axis, by)}, core)

    sibling = (ctx, dp + 1 - 2 * core)

    def remote(src, dst, send, recv, to):
        return pltpu.make_async_remote_copy(
            src_ref=src, dst_ref=dst, send_sem=send, recv_sem=recv, device_id=to, device_id_type=MESH
        )

    mine = place(**here) + (core,)
    own = wg.at[mine]
    for src, first, to, size in ((win_hbm, HEAD, K, 2), (win_hbm, 0, Q, 1), (win_hbm, 3 * HEAD, GATE, 1), (wout_hbm, 0, OUT, 1)):
        src = src.at[:, :, pl.ds(first, size * HEAD)]
        pltpu.make_async_copy(src, wg.at[mine + (EVERY, EVERY, pl.ds(to * HEAD, size * HEAD))], load_sem.at[2]).start()
    load_x = pltpu.make_async_copy(x_hbm, xv, load_sem.at[0])
    load_u = pltpu.make_async_copy(u_hbm, uv, load_sem.at[1])
    load_x.start()
    load_u.start()

    greeted = [peer(axis, by) for axis in "xyz" for by in (1, 2, 3)] + [sibling]
    barrier = pltpu.get_barrier_semaphore()
    for to in greeted:
        pl.semaphore_signal(barrier, inc=1, device_id=to, device_id_type=MESH)
    pl.semaphore_wait(barrier, len(greeted))

    def send(src, dst, send_sem, recv_sem, to):
        remote(src, dst, send_sem, recv_sem, to).start()

    def arrived(ref, recv_sem):
        remote(ref, ref, ag_s.at[0], recv_sem, sibling).wait_recv()

    def sent(ref, send_sem):
        remote(ref, ref, send_sem, ag_r.at[0, 0], sibling).wait_send()

    def w_at(n, **fixed):
        rows, lanes, _ = PIECES[n]
        return wg.at[place(**fixed) + (core, rows, EVERY, lanes)]

    W_BYTES = ((slice(0, 3), 0, 0, 0), (slice(0, 3), 0, EVERY, 0), None,
               (slice(0, 2), EVERY, EVERY, EVERY), (0, EVERY, EVERY, EVERY), (EVERY, EVERY, EVERY, EVERY))

    def ag_send(n, step, to, **fixed):
        send(w_at(n, **fixed), w_at(n, **fixed), ag_s.at[step], ag_r.at[n, step], to)

    def ag_wait(n, step):
        rows, lanes, _ = PIECES[n]
        arrived(wg.at[W_BYTES[step] + (0, rows, EVERY, lanes)], ag_r.at[n, step])

    def ag_first(n):
        axis = ORDERS[n % 3][0]
        for by in (1, 3, 2):
            ag_send(n, 0, peer(axis, by), **here)

    def ag_both(n, k):
        order = ORDERS[n % 3]
        axis, fixed = order[k], {a: here[a] for a in order[k:]}
        for by in (1, 3, 2) if k in DIRECT else (1, 3):
            ag_send(n, 2 * k - 1, peer(axis, by), **fixed)
        if k == 2:
            ag_send(n, 5, sibling, **fixed)

    def ag_relay(n, k):
        order = ORDERS[n % 3]
        axis, fixed = order[k], {a: here[a] for a in order[k:]}
        split = order[0] if k == 1 else SPLIT[axis]
        ag_wait(n, 2 * k - 1)
        for by, side in () if k in DIRECT else ((1, 0), (3, 1)):
            ag_send(n, 2 * k, peer(axis, by), half=(split, side), **{**fixed, axis: shifted(axis, 4 - by)})
        if k == 2:
            for by in (1, 3, 2) if k in DIRECT else (1, 3):
                ag_send(n, 5, sibling, **{**fixed, axis: shifted(axis, by)})

    def ag_opposite(n):
        axis = ORDERS[n % 3][2]
        ag_wait(n, 4)
        ag_send(n, 5, sibling, **{axis: shifted(axis, 2)})

    def ag_done(n):
        ag_wait(n, 5)

    pltpu.make_async_copy(own, own, load_sem.at[2]).wait()
    for n in KV + QGO:
        ag_first(n)

    rate = rate_ref[...]
    row = lax.broadcasted_iota(jnp.int32, (ROWS, HALF), 0).astype(F32)
    spacing = jnp.exp(
        lax.broadcasted_iota(jnp.int32, (1, HALF), 1).astype(F32) * (-math.log(10000.0) / HALF)
    )

    def make_tables():
        angle = (row + (ctx * ROWS).astype(F32)) * spacing
        cos_ref[...] = jnp.cos(angle)
        sin_ref[...] = jnp.sin(angle)
        up_ref[...] = jnp.exp((CENTER - row) * rate)
        down_ref[...] = jnp.exp((row - CENTER) * rate)

    rates = jnp.concatenate([rate, rate], axis=1)

    def transpose(src, dst):
        def step(c, _):
            at = pl.ds(pl.multiple_of(c * 512, 512), 512)
            dst[lax.div(c, 2), lax.rem(c, 2)] = src[:, at].T.reshape(4, 2, 2, 32, ROWS)
            return _
        lax.fori_loop(0, 8, step, 0)

    make_tables()
    for n in KV:
        ag_wait(n, 0)
        ag_both(n, 1)
    for n in QGO:
        ag_wait(n, 0)
        ag_both(n, 1)
    for n in KV:
        ag_wait(n, 1)
        ag_both(n, 2)
    load_x.wait()
    transpose(xv, xt)
    for n in KV:
        ag_relay(n, 2)
    for n in QGO:
        ag_wait(n, 1)
        ag_both(n, 2)
    load_u.wait()
    transpose(uv, ut)
    for n in KV:
        ag_opposite(n)

    def project(g):
        left = uv if g == OUT else xv
        pr[g] = dot(left[...], wg[..., lanes_of(g)].reshape(WIDTH, HEAD), 1, 0)

    def rotated(a):
        a = a.astype(BF16).astype(F32)
        a1, a2 = a[:, :HALF], a[:, HALF:]
        cos, sin = cos_ref[...], sin_ref[...]
        return jnp.concatenate([a1 * cos - a2 * sin, a1 * sin + a2 * cos], axis=1).astype(BF16).astype(F32)

    def unrotated(g):
        g1, g2 = g[:, :HALF], g[:, HALF:]
        cos, sin = cos_ref[...], sin_ref[...]
        return jnp.concatenate([g1 * cos + g2 * sin, g2 * cos - g1 * sin], axis=1).astype(BF16)

    def twice(t):
        return jnp.concatenate([t, t], axis=1)

    x_low = lax.rem(ctx, 2)
    pair_at = (ctx + 1 - 2 * x_low, dp)
    my_half, pair_half = pl.ds(128 * x_low, 128), pl.ds(128 * (1 - x_low), 128)
    shard_decay = jnp.exp(-float(ROWS) * rates)
    pair_decay = jnp.exp(-2.0 * ROWS * rates)

    class Exchange:
        def __init__(self, own, other, along_y, total, send_sem, recv_sem, backward):
            self.own, self.other, self.along_y, self.total = own, other, along_y, total
            self.s, self.r = send_sem, recv_sem
            self.hears, self.tells = (x_low == 0, x_low == 1) if backward else (x_low == 1, x_low == 0)
            self.backward = backward
            self.to_pair = remote(own.at[pair_half], other.at[pair_half], self.s.at[0], self.r.at[0], pair_at)
            self.to_pair_rest = remote(own.at[my_half], other.at[my_half], self.s.at[1], self.r.at[1], pair_at)
            self.halves = remote(total.at[my_half], total.at[my_half], self.s.at[2], self.r.at[2], pair_at)

        def each_y(self, act):
            for d in range(1, 4):
                to = here["y"] - d if self.backward else here["y"] + d

                @pl.when(to >= 0 if self.backward else to < 4)
                def _():
                    act(remote(self.along_y.at[here["y"]], self.along_y.at[here["y"]], self.s.at[2 + d],
                               self.r.at[3 + here["y"]], (to * 2 + x_low, dp)))

        def first(self):
            self.to_pair.start()
            pl.when(self.tells)(self.to_pair_rest.start)

        def second(self):
            self.to_pair.wait_recv()
            mine, theirs = self.own[my_half, :].astype(F32), self.other[my_half, :].astype(F32)
            near, away = jnp.where(self.tells, theirs, mine), jnp.where(self.tells, mine, theirs)
            self.along_y[here["y"]] = (shard_decay * away + near).astype(BF16)
            self.each_y(lambda copy: copy.start())

        def third(self):
            acc_ref[...] = jnp.zeros_like(acc_ref)

            def take(k, _):
                i = 3 - k if self.backward else k
                arrived(self.along_y.at[i], self.r.at[3 + i])
                acc_ref[...] = acc_ref[...] * pair_decay + self.along_y[i].astype(F32)
                return _

            lax.fori_loop(0, 3 - here["y"] if self.backward else here["y"], take, 0)
            self.total[my_half, :] = acc_ref[...].astype(BF16)
            self.halves.start()

        def result(self):
            self.halves.wait_recv()
            pl.when(self.hears)(self.to_pair_rest.wait_recv)
            total = self.total[...].astype(F32)
            return jnp.where(self.hears, shard_decay * total + self.other[...].astype(F32), total)

        def sent(self):
            self.to_pair.wait_send()
            pl.when(self.tells)(self.to_pair_rest.wait_send)
            self.each_y(lambda copy: copy.wait_send())
            self.halves.wait_send()

    states = Exchange(st, st_pair, st_y, st_sum, st_s, st_r, False)
    grad_states = Exchange(gs, gs_pair, gs_y, gs_sum, gs_s, gs_r, True)

    ag_done(0)
    ag_done(1)
    project(K)
    ks_ref[...] = (rotated(pr[K]) * twice(down_ref[...])).astype(BF16)
    ag_done(2)
    project(V)
    v_ref[...] = pr[V].astype(BF16)
    st[...] = (dot(v_ref[...], ks_ref[...], 0, 0) * jnp.exp(-(CENTER - 1.0) * rates)).astype(BF16)
    states.first()
    for n in QGO:
        ag_relay(n, 2)
    states.second()
    for n in QGO:
        ag_opposite(n)
    states.third()
    ag_done(3)
    project(Q)
    qs_ref[...] = (rotated(pr[Q]) * twice(up_ref[...])).astype(BF16)
    before = lax.broadcasted_iota(jnp.int32, (ROWS, ROWS), 0) >= lax.broadcasted_iota(jnp.int32, (ROWS, ROWS), 1)
    score_ref[...] = jnp.where(before, dot(qs_ref[...], ks_ref[...], 1, 1), 0.0).astype(BF16)
    ag_done(4)
    project(GATE)
    state = (states.result() * jnp.exp(-(CENTER + 1.0) * rates)).astype(BF16)
    retained = dot(score_ref[...], v_ref[...], 1, 0) + dot(qs_ref[...], state, 1, 1)
    inverse = lax.rsqrt(jnp.mean(retained * retained, axis=1, keepdims=True) + EPSILON)
    normed = retained * inverse

    ag_done(5)
    project(OUT)
    gate = pr[GATE].astype(BF16).astype(F32)
    grad_hidden = pr[OUT]
    sig = jax.nn.sigmoid(gate)
    hid_ref[...] = (gate * sig * normed).astype(BF16)
    grad_normed = grad_hidden * gate * sig
    gp[:, lanes_of(GATE)] = (grad_hidden * normed * sig * (1.0 + gate * (1.0 - sig))).astype(BF16)
    gret_ref[...] = (
        inverse * (grad_normed - normed * jnp.mean(grad_normed * normed, axis=1, keepdims=True))
    ).astype(BF16)

    gs[...] = (dot(gret_ref[...], qs_ref[...], 0, 0) * jnp.exp(-float(CENTER) * rates)).astype(BF16)
    grad_states.first()

    def half_term(g, c, of_core):
        left = ut if g == OUT else xt
        right = hid_ref[...] if g == OUT else gp[:, lanes_of(g)]
        return dot(left[pl.ds(2 * c, 2), :, :, :, of_core].reshape(1024, ROWS), right, 1, 0).reshape(2, 2, 4, 2, 2, 16, HEAD)

    def term(g):
        def step(c, _):
            pb[pl.ds(2 * c, 2), ..., lanes_of(g)] = half_term(g, c, 1 - core).astype(BF16)
            return _

        lax.fori_loop(0, 2, step, 0)
        lanes = pl.ds(g * HEAD, HEAD)
        at = (EVERY,) * 6 + (lanes,)
        send(pb.at[at], sb.at[at], sib_s.at[0], sib_r.at[g], sibling)

    def pair(g):
        arrived(sb.at[(EVERY,) * 6 + (pl.ds(g * HEAD, HEAD),)], sib_r.at[g])

        def step(c, _):
            at = (pl.ds(2 * c, 2),) + (EVERY,) * 5 + (lanes_of(g),)
            sb[at] = (half_term(g, c, core) + sb[at].astype(F32)).astype(BF16)
            return _

        lax.fori_loop(0, 2, step, 0)

    def s_idx(n, **fixed):
        rows, lanes, _ = PIECES[n]
        return place(**fixed) + (rows, EVERY, lanes)

    def rs_axis(n, k):
        a1, a2, a3 = ORDERS[n % 3]
        if k == 0:
            return a3, SPLIT[a3], {}, far_a[n], near_a[n]
        return a2, a1, {a3: here[a3]}, far_b[n], near_b[n]

    def half_of(n, k, side):
        axis, split, _, far, _ = rs_axis(n, k)
        half = pl.ds(side, 1) if split == "x" else pl.ds(2 * side, 2)
        return far.at[(EVERY, half) if split == "x" or (k == 0 and axis == "y") else (half,)]

    def rs_first(n, k):
        axis, split, fixed, _, near = rs_axis(n, k)
        if k in DIRECT_BACK:
            for slot, by in enumerate((1, 3, 2)):
                src = sb.at[s_idx(n, **{**fixed, axis: shifted(axis, by)})]
                send(src, near.at[slot], rs_s.at[2 * k + 1], rs_r.at[n, 2 * k + 1], peer(axis, by))
            return
        far = shifted(axis, 2)
        for side, by in ((0, 1), (1, 3)):
            src = sb.at[s_idx(n, half=(split, side), **{**fixed, axis: far})]
            send(src, half_of(n, k, side), rs_s.at[2 * k], rs_r.at[n, 2 * k], peer(axis, by))

    def rs_second(n, k):
        axis, split, fixed, far, near = rs_axis(n, k)
        if k in DIRECT_BACK:
            return
        arrived(far, rs_r.at[n, 2 * k])
        for side, by in ((0, 1), (1, 3)):
            at = s_idx(n, half=(split, side), **{**fixed, axis: shifted(axis, by)})
            sb[at] = (sb[at].astype(F32) + half_of(n, k, side)[...].astype(F32)).astype(BF16)
            send(sb.at[s_idx(n, **{**fixed, axis: shifted(axis, by)})], near.at[side],
                 rs_s.at[2 * k + 1], rs_r.at[n, 2 * k + 1], peer(axis, by))

    def rs_third(n, k):
        axis, _, fixed, _, near = rs_axis(n, k)
        arrived(near, rs_r.at[n, 2 * k + 1])
        at = s_idx(n, **{**fixed, axis: here[axis]})
        total = sb[at].astype(F32)
        for slot in range(near.shape[0]):
            total += near[slot].astype(F32)
        sb[at] = total.astype(BF16)
        if k == 0:
            rs_first(n, 1)
            return
        a1 = ORDERS[n % 3][0]
        for k, by in enumerate((1, 3, 2)):
            src = sb.at[s_idx(n, **{**here, a1: shifted(a1, by)})]
            send(src, last[n].at[k], rs_s.at[4], rs_r.at[n, 4], peer(a1, by))

    def rs_end(n):
        rows, lanes, to = PIECES[n]
        arrived(last[n], rs_r.at[n, 4])
        total = sb[s_idx(n, **here)].astype(F32)
        for k in range(3):
            total += last[n][k].astype(F32)
        total = total.reshape(-1, total.shape[-1])
        out_rows = EVERY if rows == EVERY else slice(16 * rows, 16 * rows + 16)
        if to is None:
            gwout_ref[out_rows, :] = total
        else:
            gwin_ref[out_rows, slice(to, to + total.shape[-1])] = total

    puts = []

    def grad_input(c):
        slot = c % 2
        if c >= 2:
            puts[c - 2].wait()
        stage[slot] = dot(gp[...], wg[c, ..., slice(0, 4 * HEAD)].reshape(1024, 4 * HEAD), 1, 1).astype(BF16)
        put = pltpu.make_async_copy(stage.at[slot], gin_hbm.at[:, pl.ds(c * 1024, 1024)], out_sem.at[slot])
        put.start()
        puts.append(put)

    term(OUT)
    term(GATE)
    grad_states.second()
    score_grad = jnp.where(before, dot(gret_ref[...], v_ref[...], 1, 1), 0.0).astype(BF16)
    grad_q = dot(score_grad, ks_ref[...], 1, 0) + dot(gret_ref[...], state, 1, 0)
    gp[:, lanes_of(Q)] = unrotated(grad_q * twice(up_ref[...]))
    term(Q)
    grad_states.third()
    pair(OUT)
    rs_first(5, 0)
    pair(GATE)
    rs_first(4, 0)
    pair(Q)
    rs_first(3, 0)
    pr[K] = dot(score_grad, qs_ref[...], 0, 0)
    rs_second(5, 0)
    rs_second(4, 0)
    grad_state = (grad_states.result() * jnp.exp(-float(CENTER) * rates)).astype(BF16)
    gp[:, lanes_of(K)] = unrotated((pr[K] + dot(v_ref[...], grad_state, 1, 0)) * twice(down_ref[...]))
    term(K)
    rs_second(3, 0)
    pr[V] = dot(score_ref[...], gret_ref[...], 0, 0)
    gp[:, lanes_of(V)] = (pr[V] + dot(ks_ref[...], grad_state, 1, 1)).astype(BF16)
    term(V)
    pair(K)
    pair(V)
    rs_first(0, 0)
    rs_first(1, 0)
    rs_first(2, 0)
    rs_third(5, 0)
    rs_third(4, 0)
    rs_third(3, 0)
    grad_input(0)
    rs_second(0, 0)
    rs_second(1, 0)
    rs_second(2, 0)
    grad_input(1)
    rs_third(5, 1)
    rs_third(4, 1)
    rs_third(3, 1)
    grad_input(2)
    rs_third(0, 0)
    rs_third(1, 0)
    rs_third(2, 0)
    rs_end(5)
    rs_end(4)
    rs_end(3)
    grad_input(3)
    rs_third(0, 1)
    rs_third(1, 1)
    rs_third(2, 1)
    rs_end(0)
    rs_end(1)
    rs_end(2)
    for put in puts[2:]:
        put.wait()
    for step, of in enumerate(W_BYTES):
        if of is not None:
            sent(wg.at[of + (0,)], ag_s.at[step])
    sent(sb, sib_s.at[0])
    for step, of in enumerate(((0,), (slice(0, 2),), None, (slice(0, 3), 0, EVERY, 0), (slice(0, 3), 0, 0, 0))):
        if of is not None:
            sent(sb.at[of], rs_s.at[step])
    states.sent()
    grad_states.sent()


def publish(a, b, c, a_out, b_out, c_out, a_held, b_held, c_held, in_sem, out_sem):
    ways = [(b, b_held, b_out), (c, c_held, c_out)]
    for k in range(4):
        rows = pl.ds(k * ROWS // 4, ROWS // 4)
        ways.append((a.at[rows], a_held.at[rows], a_out.at[rows]))
    loads = [pltpu.make_async_copy(src, held, in_sem.at[k]) for k, (src, held, _) in enumerate(ways)]
    stores = [pltpu.make_async_copy(held, dst, out_sem.at[k]) for k, (_, held, dst) in enumerate(ways)]
    for load in loads:
        load.start()
    for load, store in zip(loads, stores):
        load.wait()
        store.start()
    for store in stores:
        store.wait()


def on_device(layer_input, grad_out, w_in, w_out_t, decay_rate):
    hbm, vmem = pl.BlockSpec(memory_space=pl.ANY), pl.BlockSpec(memory_space=pltpu.VMEM)
    dma = pltpu.SemaphoreType.DMA
    buf = pltpu.VMEM
    axis_of = [ORDERS[n % 3][2] for n in range(6)]
    results = (
        jax.ShapeDtypeStruct((ROWS, WIDTH), BF16),
        jax.ShapeDtypeStruct((32, 4 * HEAD), F32),
        jax.ShapeDtypeStruct((32, HEAD), F32),
    )
    held = pl.pallas_call(
        body,
        out_shape=results,
        in_specs=[hbm, hbm, hbm, hbm, vmem],
        out_specs=(hbm, vmem, vmem),
        scratch_shapes=[
            buf((ROWS, WIDTH), BF16),
            buf((ROWS, WIDTH), BF16),
            buf((4, 2, 4, 2, 2, 32, ROWS), BF16),
            buf((4, 2, 4, 2, 2, 32, ROWS), BF16),
            buf((4, 2, 4, 2, 2, 2, 16, 5 * HEAD), BF16),
            buf((5, ROWS, HEAD), F32),
            buf((4, 2, 4, 2, 2, 16, 5 * HEAD), BF16),
            buf((4, 2, 4, 2, 2, 16, 5 * HEAD), BF16),
            buf((ROWS, 4 * HEAD), BF16),
            buf((ROWS, HALF), F32), buf((ROWS, HALF), F32), buf((ROWS, HALF), F32), buf((ROWS, HALF), F32),
            buf((ROWS, HEAD), BF16), buf((ROWS, HEAD), BF16), buf((ROWS, HEAD), BF16),
            buf((ROWS, ROWS), BF16),
            buf((HEAD // 2, HEAD), F32),
            *[buf(dims, BF16) for dims in ((HEAD, HEAD), (HEAD, HEAD), (4, HEAD // 2, HEAD), (HEAD, HEAD)) * 2],
            buf((ROWS, HEAD), BF16), buf((ROWS, HEAD), BF16),
            buf((2, ROWS, 1024), BF16),
            *[buf(BLOCK_DIMS[axis_of[n]] + inner(n), BF16) for n in range(6)],
            *[buf((2,) + BLOCK_DIMS[axis_of[n]] + inner(n), BF16) for n in range(6)],
            *[buf(PART_DIMS[axis_of[n]] + inner(n), BF16) for n in range(6)],
            *[buf((3,) + PART_DIMS[axis_of[n]] + inner(n), BF16) for n in range(6)],
            *[buf((3,) + inner(n), BF16) for n in range(6)],
            dma((6,)), dma((6, 6)),
            dma((6,)), dma((7,)), dma((6,)), dma((7,)),
            dma((1,)), dma((5,)),
            dma((5,)), dma((6, 5)),
            dma((3,)), dma((2,)),
        ],
        compiler_params=pltpu.CompilerParams(
            collective_id=0, has_side_effects=True, vmem_limit_bytes=62 * 1024 * 1024
        ),
        cost_estimate=pl.CostEstimate(flops=17 * 10**9, bytes_accessed=13 * 10**6, transcendentals=10**6),
        name="retention_backward",
    )(layer_input[0], grad_out[0], w_in.reshape(2, 16, 4 * HEAD), w_out_t.reshape(2, 16, HEAD), decay_rate[None, :])
    grad_in, grad_w, grad_wo = pl.pallas_call(
        publish, out_shape=results, in_specs=[hbm] * 3, out_specs=(hbm,) * 3, scratch_shapes=[*[buf(r.shape, r.dtype) for r in results], dma((6,)), dma((6,))], name="publish",
    )(*held)
    return grad_in[None], grad_w, grad_wo


def solution(mesh):
    rows = P(("ctx", "dp"), None)
    tokens = P("dp", "ctx", None)
    return jax.shard_map(
        on_device,
        mesh=mesh,
        in_specs=(tokens, tokens, rows, rows, P()),
        out_specs=(tokens, rows, rows),
        check_vma=False,
    )
```
